1024 devices in a mesh: expert: 64 (over y, z), dp: 16 (over x, core).
Axes of the slice: x: 8, y: 8, z: 8, core: 2. Of those that a mesh axis runs over, the one named last changes fastest.
Arguments:
- tokens: bfloat16 [8192, 1664], P('expert', 'dp'), may hold values from -6 to 6
- cotangent: bfloat16 [8192, 1664], P('expert', 'dp'), may hold values from -6 to 6
- routes: int32 [8192, 2], P('expert'), may hold values from 0 to 63, all different within a row; in each aligned block of 128 rows (0 to 127, 128 to 255, ...) at most 8 rows name the same one
- router: bfloat16 [1664, 64], replicated, may hold values from -3 to 3
- w_in: bfloat16 [64, 1664, 8192], P('expert', None, 'dp'), may hold values from -0.15625 to 0.15625
- w_out: bfloat16 [64, 8192, 1664], P('expert', 'dp'), may hold values from -0.0625 to 0.0625
Outputs:
- mixed: bfloat16 [8192, 1664], P('expert', 'dp')
- token_grad: bfloat16 [8192, 1664], P('expert', 'dp')
- router_grad: float32 [1664, 64], P('dp')
The draws below stay inside these ranges and needn't reach their ends.
Inputs may be any that keep to these rules, and one draw needn't show every extreme that they name: Each token names two different experts. Among the 256 routes of one index of expert, no expert is named more than 8 times, a bound that some block reaches.
All inputs are finite; a program needn't handle non-finite values.
Results may differ from the reference program's by a relative error of at most 0.035.
Values may be sent and summed in bfloat16 or wider, within the bound.
No kernel may reach another device: no remote copies, remote signals or barrier semaphores. Data moves between devices by JAX's collectives and lax.ppermute only.
A program may use at most 32 MiB of HBM per device.

```python
import math
import jax
import jax.numpy as jnp
import numpy as np
from jax import lax

D = 1664
FF = 8192
TOK_DEV = 128
EXPERTS = 64
TOKENS = 8192
CAP = 8
FF_DEV = 512
N_EXPERT = 64
N_DP = 16


def shared_tokens(key):
    return jnp.clip(jax.random.normal(key, (TOKENS, D), jnp.float32), -6.0, 6.0)


def draw_tokens(key, part):
    base = shared_tokens(key)
    return base.astype(jnp.bfloat16)


def draw_router(key, part):
    key = jax.random.fold_in(key, 5)
    first_key = jax.random.fold_in(key, 0)
    weights = jnp.clip(jax.random.normal(first_key, (D, EXPERTS), jnp.float32), -6.0, 6.0) * D ** (-0.5)
    return weights.astype(jnp.bfloat16)


def block_levels(stream_key, extent, pieces, smallest, largest):
    def one(dim, blocks):
        steps = jax.random.uniform(jax.random.fold_in(jax.random.fold_in(stream_key, 6), dim), (blocks,), jnp.float32, smallest / len(pieces), largest / len(pieces))
        return jnp.repeat(jnp.exp(steps), extent[dim] // blocks).reshape((-1,) + (1,) * (len(extent) - dim - 1))

    gain = one(*pieces[0])
    for cut in pieces[1:]:
        gain = gain * one(*cut)
    return gain


def routed_block(key, own, number, rows, number_of, top, reach, skew):
    ranking = jax.random.permutation(key, number_of)
    crowded, ordinary = shares(number_of, rows * top, reach, skew, True), shares(number_of, rows * top, reach, skew, False)
    places = jnp.arange(number_of)

    def named(tallies, offset_by):
        used = int((tallies > 0).sum())
        fixed = max(1, used // 4)
        passed = fixed + (places - fixed + offset_by * (used - fixed)) % max(1, number_of - fixed)
        return jnp.zeros((number_of,), jnp.int32).at[ranking[jnp.where(places < fixed, places, passed)]].set(jnp.asarray(tallies, jnp.int32))

    tallies = jnp.where(number % 4 == 0, named(crowded, number // 4), named(ordinary, number - number // 4 - 1))
    mixed = jax.random.permutation(jax.random.fold_in(own, 3), number_of)
    giver, taker = mixed[0:number_of // 2 * 2:2], mixed[1:number_of // 2 * 2:2]
    room = jnp.minimum(tallies[giver] - 1, reach - tallies[taker]) // 2
    room = jnp.where((giver == ranking[0]) | (taker == ranking[0]) | (tallies[taker] == 0), 0, jnp.maximum(room, 0))
    passed = jax.random.randint(jax.random.fold_in(own, 4), (number_of // 2,), 0, 1 << 20) % (room + 1)
    tallies = tallies.at[giver].add(-passed).at[taker].add(passed)
    labels = jnp.searchsorted(jnp.cumsum(tallies), jnp.arange(rows * top), side="right").astype(jnp.int32)
    table = labels.reshape(top, rows).T
    table = table[jax.random.permutation(jax.random.fold_in(own, 1), rows)]
    offset_by = jax.random.randint(jax.random.fold_in(own, 2), (rows, 1), 0, top)
    return jnp.take_along_axis(table, (jnp.arange(top)[None, :] + offset_by) % top, axis=1)


def shares(count, total, limit, skew, full):
    portions = [(1 << 20) // math.isqrt(grade ** skew) + 1 for grade in range(1, count + 1)]
    largest = limit if full else min(limit, max(-(-total // count), total * portions[0] // sum(portions)))
    least = 1 if total - largest >= count - 1 else 0
    counts, surplus = [largest] + [least] * (count - 1), total - largest - least * (count - 1)
    while surplus > 0:
        movable = [i for i in range(1, count) if counts[i] < largest] or [i for i in range(1, count) if counts[i] < limit]
        whole, left = sum([portions[i] for i in movable]), surplus
        for i in movable:
            more = min(limit - counts[i], max(1, left * portions[i] // whole), surplus)
            counts[i] = counts[i] + more
            surplus = surplus - more
    return np.array(counts)


def bell_draw(own_key, shape, scale, bound, cuts=(), kind=jnp.bfloat16):
    loudness = block_levels(own_key, shape, cuts, -0.22, 0.18) if cuts else 1.0
    entries = jax.random.normal(own_key, shape, jnp.float32) * scale * loudness
    return jnp.minimum(jnp.maximum(entries, -bound), bound).astype(kind)


def setup_inputs(seed: int = 0) -> dict:
    key_of = jax.random.split(jax.random.key(seed), 7)
    tokens = draw_tokens(jax.random.fold_in(key_of[6], 71), 0)
    cotangent = bell_draw(key_of[1], (TOKENS, D), 1.0, 6.0, ((0, 64), (1, 16)))
    routes_keys = jax.random.split(jax.random.fold_in(key_of[2], 1), TOKENS // TOK_DEV)
    routes_turns = jax.random.permutation(jax.random.fold_in(key_of[2], 3), TOKENS // TOK_DEV)
    routes = jax.vmap(lambda own, number: routed_block(jax.random.fold_in(key_of[2], 2), own, number, TOK_DEV, EXPERTS, 2, CAP, 2))(routes_keys, routes_turns).reshape((TOKENS, 2))
    router = draw_router(jax.random.fold_in(key_of[6], 71), 0)
    w_in = bell_draw(key_of[4], (EXPERTS, D, FF), D ** -0.5, 0.15625, ((0, 64), (2, 16)))
    w_out = bell_draw(key_of[5], (EXPERTS, FF, D), FF ** -0.5, 0.0625, ((0, 64), (1, 16)))
    return dict(tokens=tokens, cotangent=cotangent, routes=routes, router=router, w_in=w_in, w_out=w_out)


def gelu_grad(preact, upstream):
    return jax.vjp(jax.nn.gelu, preact)[1](upstream)[0]

def round_half(values):
    return lax.optimization_barrier(values.astype(jnp.bfloat16)).astype(jnp.float32)

def reference(tokens, cotangent, routes, router, w_in, w_out):
    flat_routes = routes.reshape(-1).astype(jnp.int32)
    one_hot = (flat_routes[:, None] == jnp.arange(EXPERTS, dtype=jnp.int32)[None, :]).astype(jnp.int32)
    running = jnp.cumsum(one_hot.reshape(N_EXPERT, 2 * TOK_DEV, EXPERTS), axis=1).reshape(2 * TOKENS, EXPERTS)
    slot_rank = (lax.optimization_barrier(jnp.sum(running * one_hot, axis=1)) - 1).astype(jnp.int32)
    source_block = (jnp.arange(2 * TOKENS, dtype=jnp.int32) // (2 * TOK_DEV)).astype(jnp.int32)
    slot_total = N_EXPERT * CAP
    position = (source_block * CAP + slot_rank).astype(jnp.int32)
    slot_table = jnp.full((EXPERTS, slot_total), 2 * TOKENS, jnp.int32)
    slot_table = slot_table.at[flat_routes, position].set(jnp.arange(2 * TOKENS, dtype=jnp.int32))
    pair_tokens = jnp.concatenate([jnp.repeat(tokens, 2, axis=0), jnp.zeros((1, D), jnp.bfloat16)], axis=0)
    pair_cot = jnp.concatenate([jnp.repeat(cotangent, 2, axis=0), jnp.zeros((1, D), jnp.bfloat16)], axis=0)

    def per_expert(router_acc, expert_id):
        pair_ids = slot_table[expert_id]
        slot_tokens = pair_tokens[pair_ids]
        slot_cot = pair_cot[pair_ids]
        scores = jnp.dot(slot_tokens, router, preferred_element_type=jnp.float32)
        chances = jax.nn.softmax(scores, axis=-1)
        own_expert = (jnp.arange(EXPERTS, dtype=jnp.int32) == expert_id).astype(jnp.float32)
        gating = lax.optimization_barrier(jnp.sum(chances * own_expert[None, :], axis=1))
        first_w = w_in[expert_id]
        second_w = w_out[expert_id]
        preact = jnp.dot(slot_tokens, first_w, preferred_element_type=jnp.float32)
        hidden = jax.nn.gelu(preact).astype(jnp.bfloat16)
        grad_proj = lax.dot_general(slot_cot, second_w, (((1,), (1,)), ((), ())), preferred_element_type=jnp.float32)
        hidden_blocks = hidden.astype(jnp.float32).reshape(slot_total, N_DP, FF_DEV)
        out_blocks = second_w.astype(jnp.float32).reshape(N_DP, FF_DEV, D)
        out_terms = gating[None, :, None] * jnp.einsum('rbf,bfd->brd', hidden_blocks, out_blocks)
        expert_out = lax.optimization_barrier(jnp.sum(round_half(out_terms), axis=0)).astype(jnp.bfloat16)
        gate_terms = lax.optimization_barrier(jnp.sum(hidden_blocks * grad_proj.reshape(slot_total, N_DP, FF_DEV), axis=2))
        gate_grad = lax.optimization_barrier(jnp.sum(round_half(gate_terms), axis=1))
        pre_grad = gelu_grad(preact, gating[:, None] * grad_proj).astype(jnp.bfloat16)
        in_blocks = first_w.astype(jnp.float32).reshape(D, N_DP, FF_DEV)
        back_terms = jnp.einsum('rbf,dbf->brd', pre_grad.astype(jnp.float32).reshape(slot_total, N_DP, FF_DEV), in_blocks)
        back_sum = lax.optimization_barrier(jnp.sum(round_half(back_terms), axis=0))
        score_grad = ((gate_grad * gating)[:, None] * (own_expert[None, :] - chances)).astype(jnp.bfloat16)
        router_back = lax.dot_general(score_grad, router, (((1,), (1,)), ((), ())), preferred_element_type=jnp.float32)
        expert_grad = (back_sum + router_back).astype(jnp.bfloat16)
        router_acc = router_acc + lax.dot_general(slot_tokens, score_grad, (((0,), (0,)), ((), ())), preferred_element_type=jnp.float32)
        return (router_acc, (expert_out, expert_grad))
    router_grad, (out_all, grad_all) = lax.scan(per_expert, jnp.zeros((D, EXPERTS), jnp.float32), jnp.arange(EXPERTS, dtype=jnp.int32))
    flat_ids = slot_table.reshape(-1)
    pair_out = jnp.zeros((2 * TOKENS + 1, D), jnp.bfloat16).at[flat_ids].set(out_all.reshape(-1, D))
    pair_grad = jnp.zeros((2 * TOKENS + 1, D), jnp.bfloat16).at[flat_ids].set(grad_all.reshape(-1, D))
    pair_out = pair_out[:2 * TOKENS].reshape(TOKENS, 2, D).astype(jnp.float32)
    pair_grad = pair_grad[:2 * TOKENS].reshape(TOKENS, 2, D).astype(jnp.float32)
    mixed = (pair_out[:, 0] + pair_out[:, 1]).astype(jnp.bfloat16)
    token_grad = (pair_grad[:, 0] + pair_grad[:, 1]).astype(jnp.bfloat16)
    return (mixed, token_grad, router_grad)
```

```python
import functools

import jax
import jax.numpy as jnp
import numpy as np
from jax import lax
from jax.experimental import pallas as pl
from jax.experimental.pallas import tpu as pltpu
from jax.sharding import PartitionSpec as P

F32 = jnp.float32
BF16 = jnp.bfloat16
VMEM_LIMIT = 48 * 1024 * 1024
VMEM = pl.BlockSpec(memory_space=pltpu.VMEM)
SMEM = pl.BlockSpec(memory_space=pltpu.SMEM)


def dot(a, b, dims=((1,), (0,))):
    return lax.dot_general(a, b, (dims, ((), ())), preferred_element_type=F32)


def call(body, out_shape, in_specs, flops=10_000_000, moved=1_000_000):
    return pl.pallas_call(
        body,
        out_shape=out_shape,
        in_specs=in_specs,
        out_specs=jax.tree.map(lambda _: VMEM, out_shape),
        compiler_params=pltpu.CompilerParams(vmem_limit_bytes=VMEM_LIMIT),
        cost_estimate=pl.CostEstimate(flops=flops, bytes_accessed=moved, transcendentals=0),
    )


def place_kernel(capacity, experts, routes_ref, tok_ref, cot_ref, slots_ref, pick_ref):
    rows, width = tok_ref.shape
    slots = slots_ref.shape[0]
    routes = routes_ref[...]
    lane = lax.broadcasted_iota(jnp.int32, (rows, experts), 1)
    hot = [(routes[:, k : k + 1] == lane).astype(F32) for k in range(2)]
    before = lax.broadcasted_iota(jnp.int32, (rows, rows), 0) > lax.broadcasted_iota(
        jnp.int32, (rows, rows), 1
    )
    before = before.astype(BF16)
    first = dot(before, hot[0].astype(BF16))
    second = dot(before, hot[1].astype(BF16)) + jnp.sum(hot[0], axis=0, keepdims=True)
    rank = [
        jnp.sum(first * hot[0], axis=1, keepdims=True),
        jnp.sum(second * hot[1], axis=1, keepdims=True),
    ]
    place = lax.broadcasted_iota(jnp.int32, (rows, slots), 1)
    target = [routes[:, k : k + 1] * capacity + rank[k].astype(jnp.int32) for k in range(2)]
    pick = ((place == target[0]) | (place == target[1])).astype(F32).astype(BF16)
    pick_ref[...] = pick
    slots_ref[:, :width] = dot(pick, tok_ref[...], ((0,), (0,))).astype(BF16)
    slots_ref[:, width:] = dot(pick, cot_ref[...], ((0,), (0,))).astype(BF16)


def expert_kernel(
    hidden_width,
    experts,
    at_ref,
    got_ref,
    w_ref,
    keep_ref,
    send_ref,
    gate_ref,
    chance_ref,
    acc,
    both,
    scale,
):
    phase, step = pl.program_id(0), pl.program_id(1)
    per_step = got_ref.shape[0]
    slots = got_ref.shape[1]
    width = got_ref.shape[2] // 2
    ff = hidden_width

    @pl.when(phase == 0)
    def _():
        total = dot(got_ref[0], w_ref[0])
        for j in range(1, per_step):
            total = total + dot(got_ref[j], w_ref[j])

        @pl.when(step == 0)
        def _():
            acc[...] = total

        @pl.when(step > 0)
        def _():
            acc[...] += total

    @pl.when((phase == 0) & (step == pl.num_programs(1) - 1))
    def _():
        chunk = 64
        own = at_ref[0]

        def one(i, carry):
            rows = pl.ds(pl.multiple_of(i * chunk, chunk), chunk)
            scores = acc[rows, 2 * ff :]
            lane = lax.broadcasted_iota(jnp.int32, scores.shape, 1)
            scores = jnp.where(lane < experts, scores, -jnp.inf)
            top = jnp.max(scores, axis=1, keepdims=True)
            raised = jnp.exp(scores - top)
            chances = raised / jnp.sum(raised, axis=1, keepdims=True)
            gating = jnp.sum(jnp.where(lane == own, chances, 0.0), axis=1, keepdims=True)
            x = acc[rows, :ff]
            proj = acc[rows, ff : 2 * ff]
            c = np.float32(np.sqrt(2.0 / np.pi))
            square = x * x
            t = jnp.tanh(c * (x + 0.044715 * (square * x)))
            half = 0.5 * (1.0 + t)
            hidden = (x * half).astype(BF16)
            slope = half + 0.5 * x * (1.0 - t * t) * (c * (1.0 + 3 * 0.044715 * square))
            both[rows, :ff] = (slope * (gating * proj)).astype(BF16)
            both[rows, ff:] = hidden
            gate = jnp.sum(hidden.astype(F32) * proj, axis=1, keepdims=True)
            acc[rows, 2 * ff :] = jnp.where(lane == experts, gate, chances)
            wide = lax.broadcasted_iota(jnp.int32, (chunk, 2 * width), 1)
            scale[rows, :] = jnp.where(wide < width, 1.0, gating)
            return carry

        lax.fori_loop(0, slots // chunk, one, 0)
        turned = acc[:, 2 * ff :].T
        chance_ref[...] = turned[:experts]
        gate_ref[...] = turned[experts : experts + 8]

    @pl.when(phase == 1)
    def _():
        core = at_ref[1]
        for j in range(per_step // 2):
            for ref, which in ((keep_ref, core), (send_ref, 1 - core)):
                term = dot(both[...], w_ref[2 * j + which, :, : 2 * ff], ((1,), (1,)))
                ref[j, :, : 2 * width] = (term * scale[...]).astype(BF16)
                ref[j, :, 2 * width :] = jnp.zeros((slots, ref.shape[2] - 2 * width), BF16)


def router_kernel(experts, at_ref, gates_ref, chance_ref, slots_ref, score_ref, part_ref):
    gate = jnp.sum(gates_ref[...], axis=0, keepdims=True)
    chances = chance_ref[...]
    own = (lax.broadcasted_iota(jnp.int32, chances.shape, 0) == at_ref[0]).astype(F32)
    gating = jnp.sum(chances * own, axis=0, keepdims=True)
    score = ((gate * gating) * (own - chances)).astype(BF16)
    score_ref[...] = score
    part_ref[...] = dot(score, slots_ref[...])[:, : part_ref.shape[1]]


def fits(rows, capacity, per_row):
    row = lax.broadcasted_iota(jnp.int32, (rows, 128), 0) & (capacity - 1)
    lane = lax.broadcasted_iota(jnp.int32, (rows, 128), 1)
    return (lane >= row * per_row) & (lane < row * per_row + per_row)


def return_kernel(
    capacity, per_row, sums_ref, score_ref, router_ref, column_ref, fold_ref, out_ref
):
    rows = sums_ref.shape[0]
    width = router_ref.shape[1]
    back = dot(score_ref[...], router_ref[...], ((0,), (0,)))
    out_ref[:, :width] = (sums_ref[:, :width].astype(F32) + back).astype(BF16)
    column = jnp.sum(column_ref[...], axis=0, keepdims=True)
    high = column.astype(BF16)
    low = (column - high.astype(F32)).astype(BF16)
    mask = fits(rows, capacity, per_row)
    spread = [jnp.where(mask, part.astype(F32), 0.0).astype(BF16) for part in (high, low)]
    folded = dot(spread[0], fold_ref[0]) + dot(spread[1], fold_ref[1])
    out_ref[:, width:] = folded.astype(BF16)


def combine_kernel(
    capacity, per_row, got_ref, pick_ref, fold_ref, mixed_ref, token_ref, router_ref
):
    rows = got_ref.shape[0]
    width = mixed_ref.shape[1]
    pair = dot(pick_ref[...], got_ref[:, : 2 * width])
    token_ref[...] = pair[:, :width].astype(BF16)
    mixed_ref[...] = pair[:, width:].astype(BF16)
    tail = got_ref[:, 2 * width :]
    spread = dot(tail, fold_ref[0], ((1,), (1,))) + dot(tail, fold_ref[1], ((1,), (1,)))
    spread = jnp.where(fits(rows, capacity, per_row), spread, 0.0)
    columns = jnp.sum(spread.reshape(rows // capacity, capacity, 128), axis=1)
    router_ref[...] = columns.T[: router_ref.shape[0]]


def shards(tokens, cotangent, routes, router, w_in, w_out):
    tok_count, width = tokens.shape
    experts = router.shape[1]
    sources = lax.axis_size("expert")
    groups = lax.axis_size("dp")
    chips = groups // 2
    capacity = 8
    slots = sources * capacity
    ff = w_in.shape[2]
    tail = 48
    per_row = width // capacity
    same_core = [[2 * chip + core for chip in range(chips)] for core in range(2)]
    swap = [(index, index ^ 1) for index in range(groups)]
    dp = lax.axis_index("dp")
    at = jnp.stack([lax.axis_index("expert"), dp % 2]).astype(jnp.int32)
    fold = np.zeros((2, 128, tail), np.float32)
    for lane in range(width):
        fold[0, lane, lane % per_row] = 1
        fold[1, lane, per_row + lane % per_row] = 1
    fold = jnp.asarray(fold, BF16)

    mine, pick = call(
        functools.partial(place_kernel, capacity, experts),
        (
            jax.ShapeDtypeStruct((slots, 2 * width), BF16),
            jax.ShapeDtypeStruct((tok_count, slots), BF16),
        ),
        [VMEM] * 3,
    )(routes, tokens, cotangent)
    got = lax.all_to_all(
        mine.reshape(sources, capacity, 2 * width), "expert", split_axis=0, concat_axis=0, tiled=True
    ).reshape(slots, 2 * width)

    got, w_in, w_out, router = lax.optimization_barrier((got, w_in, w_out, router))
    whole = lax.all_gather(got[None], "dp", axis=0, tiled=True)

    front = w_in[0].reshape(groups, width, ff)
    back = w_out[0].T.reshape(groups, width, ff)
    gate_rows = jnp.pad(router.reshape(groups, width, experts), ((0, 0), (0, 0), (0, 128 - experts)))
    empty = jnp.zeros_like(front)
    weights = jnp.concatenate(
        [
            jnp.concatenate([front, empty, gate_rows], axis=2),
            jnp.concatenate([empty, back, jnp.zeros_like(gate_rows)], axis=2),
        ],
        axis=1,
    )

    per_step = 4
    steps = groups // per_step
    columns = 2 * ff + 128
    keep, send, gate_term, chances = pl.pallas_call(
        functools.partial(expert_kernel, ff, experts),
        grid_spec=pltpu.PrefetchScalarGridSpec(
            num_scalar_prefetch=1,
            grid=(2, steps),
            in_specs=[
                pl.BlockSpec(
                    (per_step, slots, 2 * width), lambda p, i, at: (i * (1 - p) + (steps - 1) * p, 0, 0)
                ),
                pl.BlockSpec((per_step, 2 * width, columns), lambda p, i, at: (i, 0, 0)),
            ],
            out_specs=[
                pl.BlockSpec((per_step // 2, slots, 256), lambda p, i, at: (i * p, 0, 0)),
                pl.BlockSpec((per_step // 2, slots, 256), lambda p, i, at: (i * p, 0, 0)),
                pl.BlockSpec((8, slots), lambda p, i, at: (0, 0)),
                pl.BlockSpec((experts, slots), lambda p, i, at: (0, 0)),
            ],
            scratch_shapes=[
                pltpu.VMEM((slots, columns), F32),
                pltpu.VMEM((slots, 2 * ff), BF16),
                pltpu.VMEM((slots, 2 * width), F32),
            ],
        ),
        out_shape=(
            jax.ShapeDtypeStruct((chips, slots, 256), BF16),
            jax.ShapeDtypeStruct((chips, slots, 256), BF16),
            jax.ShapeDtypeStruct((8, slots), F32),
            jax.ShapeDtypeStruct((experts, slots), F32),
        ),
        compiler_params=pltpu.CompilerParams(vmem_limit_bytes=VMEM_LIMIT),
        cost_estimate=pl.CostEstimate(
            flops=8_000_000_000, bytes_accessed=24_000_000, transcendentals=slots * ff
        ),
    )(at, whole, weights)

    swapped = lax.ppermute(send, "dp", swap)
    halves = (keep.astype(F32) + swapped.astype(F32)).astype(BF16)
    sums = lax.psum_scatter(
        halves, "dp", scatter_dimension=0, axis_index_groups=same_core, tiled=True
    )

    gates = lax.all_to_all(
        jnp.broadcast_to(gate_term[None, :1], (groups, 1, slots)),
        "dp",
        split_axis=0,
        concat_axis=0,
        tiled=True,
    ).reshape(groups, slots)
    score_grad, router_part = call(
        functools.partial(router_kernel, experts),
        (
            jax.ShapeDtypeStruct((experts, slots), BF16),
            jax.ShapeDtypeStruct((experts, 128), F32),
        ),
        [SMEM] + [VMEM] * 3,
    )(at, gates, chances, got)
    router_column = lax.all_to_all(
        router_part.reshape(experts, 1, 128), "expert", split_axis=0, concat_axis=0, tiled=True
    ).reshape(experts, 128)

    router_slice = lax.dynamic_slice_in_dim(router, dp * width, width, 0).T
    router_slice = jnp.pad(router_slice, ((0, 0), (0, width)))
    home = call(
        functools.partial(return_kernel, capacity, per_row),
        jax.ShapeDtypeStruct((slots, 2 * width + tail), BF16),
        [VMEM] * 5,
    )(sums.reshape(slots, 256), score_grad, router_slice, router_column, fold)
    home = lax.all_to_all(
        home.reshape(sources, capacity, 2 * width + tail),
        "expert",
        split_axis=0,
        concat_axis=0,
        tiled=True,
    ).reshape(slots, 2 * width + tail)
    mixed, token_grad, router_grad = call(
        functools.partial(combine_kernel, capacity, per_row),
        (
            jax.ShapeDtypeStruct((tok_count, width), BF16),
            jax.ShapeDtypeStruct((tok_count, width), BF16),
            jax.ShapeDtypeStruct((width, experts), F32),
        ),
        [VMEM] * 3,
    )(home, pick, fold)
    return (mixed, token_grad, router_grad)


def solution(mesh):
    placed = (
        P("expert", "dp"),
        P("expert", "dp"),
        P("expert", None),
        P(),
        P("expert", None, "dp"),
        P("expert", "dp", None),
    )
    return jax.shard_map(
        shards,
        mesh=mesh,
        in_specs=placed,
        out_specs=(P("expert", "dp"), P("expert", "dp"), P("dp", None)),
        check_vma=False,
    )
```

```python
import functools

import jax
import jax.numpy as jnp
import numpy as np
from jax import lax
from jax.experimental import pallas as pl
from jax.experimental.pallas import tpu as pltpu
from jax.sharding import PartitionSpec as P

F32 = jnp.float32
BF16 = jnp.bfloat16
LANES = 128
VMEM_LIMIT = 48 * 1024 * 1024
VMEM = pl.BlockSpec(memory_space=pltpu.VMEM)
SMEM = pl.BlockSpec(memory_space=pltpu.SMEM)


def dot(a, b, dims=((1,), (0,))):
    return lax.dot_general(a, b, (dims, ((), ())), preferred_element_type=F32)


def call(body, out_shape, in_specs, flops=10_000_000, moved=1_000_000):
    return pl.pallas_call(
        body,
        out_shape=out_shape,
        in_specs=in_specs,
        out_specs=jax.tree.map(lambda _: VMEM, out_shape),
        compiler_params=pltpu.CompilerParams(vmem_limit_bytes=VMEM_LIMIT),
        cost_estimate=pl.CostEstimate(flops=flops, bytes_accessed=moved, transcendentals=0),
    )


def place_kernel(capacity, experts, routes_ref, tok_ref, cot_ref, slots_ref, pick_ref):
    width, rows = tok_ref.shape
    slots = slots_ref.shape[0]
    routes = routes_ref[...]
    number = lax.broadcasted_iota(jnp.int32, (experts, rows), 0)
    hot = [(routes[k : k + 1] == number).astype(F32) for k in range(2)]
    before = lax.broadcasted_iota(jnp.int32, (rows, rows), 0) < lax.broadcasted_iota(
        jnp.int32, (rows, rows), 1
    )
    before = before.astype(F32).astype(BF16)
    first = dot(hot[0].astype(BF16), before)
    second = dot(hot[1].astype(BF16), before) + jnp.sum(hot[0], axis=1, keepdims=True)
    rank = [
        jnp.sum(first * hot[0], axis=0, keepdims=True),
        jnp.sum(second * hot[1], axis=0, keepdims=True),
    ]
    place = lax.broadcasted_iota(jnp.int32, (slots, rows), 0)
    target = [routes[k : k + 1] * capacity + rank[k].astype(jnp.int32) for k in range(2)]
    pick = ((place == target[0]) | (place == target[1])).astype(F32).astype(BF16)
    pick_ref[...] = pick
    blank = jnp.zeros((slots, LANES - width), BF16)
    for at, ref in ((0, tok_ref), (LANES, cot_ref)):
        slots_ref[:, at : at + width] = dot(pick, ref[...], ((1,), (1,))).astype(BF16)
        slots_ref[:, at + width : at + LANES] = blank


def terms(pre, hidden, gating, front_ref, back_ref, which, out_ref):
    pairs = out_ref.shape[0]
    offsets = [pl.multiple_of((2 * j + which) * LANES, LANES) for j in range(pairs)]
    front = jnp.concatenate([front_ref[pl.ds(at, LANES), :] for at in offsets], axis=0)
    back = jnp.concatenate([back_ref[:, pl.ds(at, LANES)] for at in offsets], axis=1)
    grad = dot(pre, front, ((1,), (1,)))
    out = dot(hidden, back)
    for j in range(pairs):
        lanes = slice(j * LANES, (j + 1) * LANES)
        out_ref[j, :, :LANES] = grad[:, lanes].astype(BF16)
        out_ref[j, :, LANES:] = (gating * out[:, lanes]).astype(BF16)


def expert_kernel(
    experts,
    at_ref,
    got_ref,
    front_ref,
    back_ref,
    router_ref,
    send_ref,
    pre_ref,
    hidden_ref,
    gating_ref,
    gate_ref,
    chance_ref,
    acc,
    proj,
    rates,
):
    phase, step = pl.program_id(0), pl.program_id(1)
    per_step, slots = got_ref.shape[0], got_ref.shape[1]

    @pl.when(phase == 0)
    def _():
        tok = jnp.concatenate([got_ref[j, :, :LANES] for j in range(per_step)], axis=1)
        cot = jnp.concatenate([got_ref[j, :, LANES:] for j in range(per_step)], axis=1)

        @pl.when(step == 0)
        def _():
            acc[...] = dot(tok, front_ref[...])
            proj[...] = dot(cot, back_ref[...], ((1,), (1,)))
            rates[...] = dot(tok, router_ref[...], ((1,), (1,)))

        @pl.when(step > 0)
        def _():
            acc[...] += dot(tok, front_ref[...])
            proj[...] += dot(cot, back_ref[...], ((1,), (1,)))
            rates[...] += dot(tok, router_ref[...], ((1,), (1,)))

    @pl.when((phase == 0) & (step == pl.num_programs(1) - 1))
    def _():
        chunk = 64
        own = at_ref[0]

        def one(i, carry):
            rows = pl.ds(pl.multiple_of(i * chunk, chunk), chunk)
            scores = rates[rows, :]
            lane = lax.broadcasted_iota(jnp.int32, scores.shape, 1)
            scores = jnp.where(lane < experts, scores, -jnp.inf)
            top = jnp.max(scores, axis=1, keepdims=True)
            raised = jnp.exp(scores - top)
            chances = raised / jnp.sum(raised, axis=1, keepdims=True)
            gating = jnp.sum(jnp.where(lane == own, chances, 0.0), axis=1, keepdims=True)
            x = acc[rows, :]
            up = proj[rows, :]
            c = np.float32(np.sqrt(2.0 / np.pi))
            square = x * x
            t = jnp.tanh(c * (x + 0.044715 * (square * x)))
            half = 0.5 * (1.0 + t)
            hidden = (x * half).astype(BF16)
            slope = half + 0.5 * x * (1.0 - t * t) * (c * (1.0 + 3 * 0.044715 * square))
            pre_ref[rows, :] = (slope * (gating * up)).astype(BF16)
            hidden_ref[rows, :] = hidden
            gate = jnp.sum(hidden.astype(F32) * up, axis=1, keepdims=True)
            rates[rows, :] = jnp.where(lane == experts, gate, chances)
            gating_ref[rows, :] = jnp.broadcast_to(gating, (chunk, LANES))
            return carry

        lax.fori_loop(0, slots // chunk, one, 0)
        turned = rates[...].T
        chance_ref[...] = turned[:experts]
        gate_ref[...] = turned[experts : experts + 8]

    @pl.when(phase == 1)
    def _():
        terms(
            pre_ref[...], hidden_ref[...], gating_ref[...], front_ref, back_ref, 1 - at_ref[1], send_ref
        )


def keep_kernel(at_ref, pre_ref, hidden_ref, gating_ref, front_ref, back_ref, keep_ref):
    terms(pre_ref[...], hidden_ref[...], gating_ref[...], front_ref, back_ref, at_ref[1], keep_ref)


def router_kernel(at_ref, gates_ref, chance_ref, slots_ref, score_ref, part_ref):
    gate = jnp.sum(gates_ref[...], axis=0, keepdims=True)
    chances = chance_ref[...]
    own = (lax.broadcasted_iota(jnp.int32, chances.shape, 0) == at_ref[0]).astype(F32)
    gating = jnp.sum(chances * own, axis=0, keepdims=True)
    score = ((gate * gating) * (own - chances)).astype(BF16)
    score_ref[...] = score
    part_ref[...] = dot(score, slots_ref[:, :LANES])


def fits(rows, capacity, per_row):
    row = lax.broadcasted_iota(jnp.int32, (rows, LANES), 0) & (capacity - 1)
    lane = lax.broadcasted_iota(jnp.int32, (rows, LANES), 1)
    return (lane >= row * per_row) & (lane < row * per_row + per_row)


def return_kernel(
    capacity, per_row, sums_ref, score_ref, router_ref, column_ref, fold_ref, out_ref
):
    rows = sums_ref.shape[0]
    back = dot(score_ref[...], router_ref[...], ((0,), (0,)))
    column = jnp.sum(column_ref[...], axis=0, keepdims=True)
    high = column.astype(BF16)
    low = (column - high.astype(F32)).astype(BF16)
    mask = fits(rows, capacity, per_row)
    high, low = [
        dot(jnp.where(mask, part.astype(F32), 0.0).astype(BF16), fold_ref[...]) for part in (high, low)
    ]
    sums = sums_ref[...].astype(F32)
    out_ref[:, :LANES] = (sums[:, :LANES] + back + high).astype(BF16)
    out_ref[:, LANES:] = (sums[:, LANES:] + low).astype(BF16)


def combine_kernel(
    capacity, per_row, got_ref, pick_ref, fold_ref, mixed_ref, token_ref, router_ref
):
    rows = got_ref.shape[0]
    width = mixed_ref.shape[0]
    got = got_ref[...]
    pair = dot(got, pick_ref[...], ((0,), (0,)))
    token_ref[...] = pair[:width].astype(BF16)
    mixed_ref[...] = pair[LANES : LANES + width].astype(BF16)
    spread = [dot(part, fold_ref[...], ((1,), (1,))) for part in (got[:, :LANES], got[:, LANES:])]
    spread = jnp.where(fits(rows, capacity, per_row), spread[0] + spread[1], 0.0)
    columns = jnp.sum(spread.reshape(rows // capacity, capacity, LANES), axis=1)
    router_ref[...] = columns[:, : router_ref.shape[1]]


def shards(tokens, cotangent, routes, router, w_in, w_out):
    tok_count, width = tokens.shape
    experts = router.shape[1]
    sources = lax.axis_size("expert")
    groups = lax.axis_size("dp")
    chips = groups // 2
    capacity = 8
    slots = sources * capacity
    ff = w_in.shape[2]
    lanes = 2 * LANES
    per_row = width // capacity
    same_core = [[2 * chip + core for chip in range(chips)] for core in range(2)]
    swap = [(index, index ^ 1) for index in range(groups)]
    dp = lax.axis_index("dp")
    at = jnp.stack([lax.axis_index("expert"), dp % 2]).astype(jnp.int32)
    fold = np.zeros((LANES, LANES), np.float32)
    for lane in range(width):
        fold[lane, width + lane % per_row] = 1
    fold = jnp.asarray(fold, BF16)

    mine, pick = call(
        functools.partial(place_kernel, capacity, experts),
        (
            jax.ShapeDtypeStruct((slots, lanes), BF16),
            jax.ShapeDtypeStruct((slots, tok_count), BF16),
        ),
        [VMEM] * 3,
    )(routes.T, tokens.T, cotangent.T)
    got = lax.all_to_all(
        mine.reshape(sources, capacity, lanes), "expert", split_axis=0, concat_axis=0, tiled=True
    ).reshape(slots, lanes)

    got, w_in, w_out, router = lax.optimization_barrier((got, w_in, w_out, router))
    whole = lax.all_gather(got[None], "dp", axis=0, tiled=True)

    spare = LANES - width
    front = jnp.pad(w_in[0].reshape(groups, width, ff), ((0, 0), (0, spare), (0, 0)))
    front = front.reshape(groups * LANES, ff)
    back = jnp.pad(w_out[0].reshape(ff, groups, width), ((0, 0), (0, 0), (0, spare)))
    back = back.reshape(ff, groups * LANES)
    scorer = jnp.pad(
        router.T.reshape(experts, groups, width), ((0, LANES - experts), (0, 0), (0, spare))
    ).reshape(LANES, groups * LANES)

    per_step = 4
    steps = groups // per_step
    depth = per_step * LANES
    send, pre, hidden, gating, gate_term, chances = pl.pallas_call(
        functools.partial(expert_kernel, experts),
        grid_spec=pltpu.PrefetchScalarGridSpec(
            num_scalar_prefetch=1,
            grid=(2, steps),
            in_specs=[
                pl.BlockSpec(
                    (per_step, slots, lanes), lambda p, i, at: (i * (1 - p) + (steps - 1) * p, 0, 0)
                ),
                pl.BlockSpec((depth, ff), lambda p, i, at: (i, 0)),
                pl.BlockSpec((ff, depth), lambda p, i, at: (0, i)),
                pl.BlockSpec((LANES, depth), lambda p, i, at: (0, i * (1 - p) + (steps - 1) * p)),
            ],
            out_specs=[
                pl.BlockSpec((per_step // 2, slots, lanes), lambda p, i, at: (i * p, 0, 0)),
                pl.BlockSpec((slots, ff), lambda p, i, at: (0, 0)),
                pl.BlockSpec((slots, ff), lambda p, i, at: (0, 0)),
                pl.BlockSpec((slots, LANES), lambda p, i, at: (0, 0)),
                pl.BlockSpec((8, slots), lambda p, i, at: (0, 0)),
                pl.BlockSpec((experts, slots), lambda p, i, at: (0, 0)),
            ],
            scratch_shapes=[
                pltpu.VMEM((slots, ff), F32),
                pltpu.VMEM((slots, ff), F32),
                pltpu.VMEM((slots, LANES), F32),
            ],
        ),
        out_shape=(
            jax.ShapeDtypeStruct((chips, slots, lanes), BF16),
            jax.ShapeDtypeStruct((slots, ff), BF16),
            jax.ShapeDtypeStruct((slots, ff), BF16),
            jax.ShapeDtypeStruct((slots, LANES), F32),
            jax.ShapeDtypeStruct((8, slots), F32),
            jax.ShapeDtypeStruct((experts, slots), F32),
        ),
        compiler_params=pltpu.CompilerParams(vmem_limit_bytes=VMEM_LIMIT),
        cost_estimate=pl.CostEstimate(
            flops=4_000_000_000, bytes_accessed=16_000_000, transcendentals=slots * ff
        ),
    )(at, whole, front, back, scorer)

    swapped = lax.ppermute(send, "dp", swap)
    keep = pl.pallas_call(
        keep_kernel,
        grid_spec=pltpu.PrefetchScalarGridSpec(
            num_scalar_prefetch=1,
            grid=(steps,),
            in_specs=[
                pl.BlockSpec((slots, ff), lambda i, at: (0, 0)),
                pl.BlockSpec((slots, ff), lambda i, at: (0, 0)),
                pl.BlockSpec((slots, LANES), lambda i, at: (0, 0)),
                pl.BlockSpec((depth, ff), lambda i, at: (i, 0)),
                pl.BlockSpec((ff, depth), lambda i, at: (0, i)),
            ],
            out_specs=pl.BlockSpec((per_step // 2, slots, lanes), lambda i, at: (i, 0, 0)),
        ),
        out_shape=jax.ShapeDtypeStruct((chips, slots, lanes), BF16),
        compiler_params=pltpu.CompilerParams(vmem_limit_bytes=VMEM_LIMIT),
        cost_estimate=pl.CostEstimate(
            flops=2_000_000_000, bytes_accessed=8_000_000, transcendentals=0
        ),
    )(at, pre, hidden, gating, front, back)
    halves = (keep.astype(F32) + swapped.astype(F32)).astype(BF16)
    halves, gate_term = lax.optimization_barrier((halves, gate_term))
    sums = lax.psum_scatter(
        halves, "dp", scatter_dimension=0, axis_index_groups=same_core, tiled=True
    )

    gates = lax.all_to_all(
        jnp.broadcast_to(gate_term[None, :1], (groups, 1, slots)),
        "dp",
        split_axis=0,
        concat_axis=0,
        tiled=True,
    ).reshape(groups, slots)
    score_grad, router_part = call(
        router_kernel,
        (
            jax.ShapeDtypeStruct((experts, slots), BF16),
            jax.ShapeDtypeStruct((experts, LANES), F32),
        ),
        [SMEM] + [VMEM] * 3,
    )(at, gates, chances, got)
    router_column = lax.all_to_all(
        router_part.reshape(experts, 1, LANES), "expert", split_axis=0, concat_axis=0, tiled=True
    ).reshape(experts, LANES)

    router_slice = lax.dynamic_slice_in_dim(router.T, dp * width, width, 1)
    router_slice = jnp.pad(router_slice, ((0, 0), (0, spare)))
    home = call(
        functools.partial(return_kernel, capacity, per_row),
        jax.ShapeDtypeStruct((slots, lanes), BF16),
        [VMEM] * 5,
    )(sums.reshape(slots, lanes), score_grad, router_slice, router_column, fold)
    home = lax.all_to_all(
        home.reshape(sources, capacity, lanes), "expert", split_axis=0, concat_axis=0, tiled=True
    ).reshape(slots, lanes)
    mixed, token_grad, router_grad = call(
        functools.partial(combine_kernel, capacity, per_row),
        (
            jax.ShapeDtypeStruct((width, tok_count), BF16),
            jax.ShapeDtypeStruct((width, tok_count), BF16),
            jax.ShapeDtypeStruct((experts, width), F32),
        ),
        [VMEM] * 3,
    )(home, pick, fold)
    return (mixed.T, token_grad.T, router_grad.T)


def solution(mesh):
    placed = (
        P("expert", "dp"),
        P("expert", "dp"),
        P("expert", None),
        P(),
        P("expert", None, "dp"),
        P("expert", "dp", None),
    )
    return jax.shard_map(
        shards,
        mesh=mesh,
        in_specs=placed,
        out_specs=(P("expert", "dp"), P("expert", "dp"), P("dp", None)),
        check_vma=False,
    )
```

```python
import functools

import jax
import jax.numpy as jnp
import numpy as np
from jax import lax
from jax.experimental import pallas as pl
from jax.experimental.pallas import tpu as pltpu
from jax.sharding import PartitionSpec as P

F32 = jnp.float32
BF16 = jnp.bfloat16
LANES = 128
VMEM_LIMIT = 24 * 1024 * 1024
VMEM = pl.BlockSpec(memory_space=pltpu.VMEM)
SMEM = pl.BlockSpec(memory_space=pltpu.SMEM)


def dot(a, b, dims=((1,), (0,))):
    return lax.dot_general(a, b, (dims, ((), ())), preferred_element_type=F32)


def call(body, out_shape, in_specs, flops=10_000_000, moved=1_000_000):
    return pl.pallas_call(
        body,
        out_shape=out_shape,
        in_specs=in_specs,
        out_specs=jax.tree.map(lambda _: VMEM, out_shape),
        compiler_params=pltpu.CompilerParams(vmem_limit_bytes=VMEM_LIMIT),
        cost_estimate=pl.CostEstimate(flops=flops, bytes_accessed=moved, transcendentals=0),
    )


def place_kernel(capacity, experts, routes_ref, tok_ref, cot_ref, slots_ref, pick_ref):
    width, rows = tok_ref.shape
    slots = slots_ref.shape[0]
    routes = routes_ref[...]
    number = lax.broadcasted_iota(jnp.int32, (experts, rows), 0)
    hot = [(routes[k : k + 1] == number).astype(F32) for k in range(2)]
    before = lax.broadcasted_iota(jnp.int32, (rows, rows), 0) < lax.broadcasted_iota(
        jnp.int32, (rows, rows), 1
    )
    before = before.astype(F32).astype(BF16)
    first = dot(hot[0].astype(BF16), before)
    second = dot(hot[1].astype(BF16), before) + jnp.sum(hot[0], axis=1, keepdims=True)
    rank = [
        jnp.sum(first * hot[0], axis=0, keepdims=True),
        jnp.sum(second * hot[1], axis=0, keepdims=True),
    ]
    place = lax.broadcasted_iota(jnp.int32, (slots, rows), 0)
    target = [routes[k : k + 1] * capacity + rank[k].astype(jnp.int32) for k in range(2)]
    pick = ((place == target[0]) | (place == target[1])).astype(F32).astype(BF16)
    pick_ref[...] = pick
    blank = jnp.zeros((slots, LANES - width), BF16)
    for at, ref in ((0, tok_ref), (LANES, cot_ref)):
        slots_ref[:, at : at + width] = dot(pick, ref[...], ((1,), (1,))).astype(BF16)
        slots_ref[:, at + width : at + LANES] = blank


def terms(at, pre_ref, hidden_ref, gating_ref, front_ref, back_ref, out_ref):
    chips = out_ref.shape[0]
    for pair in range(chips // 2):
        offsets = [
            pl.multiple_of((2 * (2 * pair + j) + at) * LANES, LANES) for j in range(2)
        ]
        front = jnp.concatenate([front_ref[pl.ds(o, LANES), :] for o in offsets], axis=0)
        back = jnp.concatenate([back_ref[:, pl.ds(o, LANES)] for o in offsets], axis=1)
        grad = dot(pre_ref[...], front, ((1,), (1,)))
        out = dot(hidden_ref[...], back)
        for j in range(2):
            lanes = slice(j * LANES, (j + 1) * LANES)
            out_ref[2 * pair + j, :, :LANES] = grad[:, lanes].astype(BF16)
            out_ref[2 * pair + j, :, LANES:] = (gating_ref[...] * out[:, lanes]).astype(BF16)


def expert_kernel(
    experts,
    at_ref,
    whole_ref,
    front_ref,
    back_ref,
    router_ref,
    send_ref,
    pre_ref,
    hidden_ref,
    gating_ref,
    gate_ref,
    chance_ref,
    got,
    acc,
    proj,
    rates,
    sems,
):
    parts = sems.shape[0]
    per_part = got.shape[0] // parts
    slots = got.shape[1]
    depth = per_part * LANES
    copies = [
        pltpu.make_async_copy(
            whole_ref.at[pl.ds(i * per_part, per_part)], got.at[pl.ds(i * per_part, per_part)], sems.at[i]
        )
        for i in range(parts)
    ]
    for copy in copies:
        copy.start()
    for i in range(parts):
        copies[i].wait()
        blocks = range(i * per_part, (i + 1) * per_part)
        tok = jnp.concatenate([got[j, :, :LANES] for j in blocks], axis=1)
        cot = jnp.concatenate([got[j, :, LANES:] for j in blocks], axis=1)
        span = slice(i * depth, (i + 1) * depth)
        new = (
            dot(tok, front_ref[span, :]),
            dot(cot, back_ref[:, span], ((1,), (1,))),
            dot(tok, router_ref[:, span], ((1,), (1,))),
        )
        for ref, value in zip((acc, proj, rates), new):
            ref[...] = value if i == 0 else ref[...] + value

    chunk = min(128, slots)
    own = at_ref[0]

    def one(i, carry):
        rows = pl.ds(pl.multiple_of(i * chunk, chunk), chunk)
        scores = rates[rows, :]
        lane = lax.broadcasted_iota(jnp.int32, scores.shape, 1)
        scores = jnp.where(lane < experts, scores, -jnp.inf)
        top = jnp.max(scores, axis=1, keepdims=True)
        raised = jnp.exp(scores - top)
        chances = raised / jnp.sum(raised, axis=1, keepdims=True)
        gating = jnp.sum(jnp.where(lane == own, chances, 0.0), axis=1, keepdims=True)
        x = acc[rows, :]
        up = proj[rows, :]
        c = np.float32(np.sqrt(2.0 / np.pi))
        square = x * x
        t = jnp.tanh(c * (x + 0.044715 * (square * x)))
        half = 0.5 * (1.0 + t)
        hidden = (x * half).astype(BF16)
        slope = half + 0.5 * x * (1.0 - t * t) * (c * (1.0 + 3 * 0.044715 * square))
        pre_ref[rows, :] = (slope * (gating * up)).astype(BF16)
        hidden_ref[rows, :] = hidden
        gate = jnp.sum(hidden.astype(F32) * up, axis=1, keepdims=True)
        rates[rows, :] = jnp.where(lane == experts, gate, chances)
        gating_ref[rows, :] = jnp.broadcast_to(gating, (chunk, LANES))
        return carry

    lax.fori_loop(0, slots // chunk, one, 0)
    turned = rates[...].T
    chance_ref[...] = turned[:experts]
    gate_ref[...] = turned[experts : experts + 8]
    terms(1 - at_ref[1], pre_ref, hidden_ref, gating_ref, front_ref, back_ref, send_ref)


def keep_kernel(at_ref, pre_ref, hidden_ref, gating_ref, front_ref, back_ref, keep_ref):
    terms(at_ref[1], pre_ref, hidden_ref, gating_ref, front_ref, back_ref, keep_ref)


def router_kernel(at_ref, gates_ref, chance_ref, slots_ref, score_ref, part_ref):
    gate = jnp.sum(gates_ref[...], axis=0, keepdims=True)
    chances = chance_ref[...]
    own = (lax.broadcasted_iota(jnp.int32, chances.shape, 0) == at_ref[0]).astype(F32)
    gating = jnp.sum(chances * own, axis=0, keepdims=True)
    score = ((gate * gating) * (own - chances)).astype(BF16)
    score_ref[...] = score
    part_ref[...] = dot(score, slots_ref[:, :LANES])


def fits(rows, capacity, per_row):
    row = lax.broadcasted_iota(jnp.int32, (rows, LANES), 0) & (capacity - 1)
    lane = lax.broadcasted_iota(jnp.int32, (rows, LANES), 1)
    return (lane >= row * per_row) & (lane < row * per_row + per_row)


def return_kernel(
    capacity, per_row, sums_ref, score_ref, router_ref, column_ref, fold_ref, out_ref
):
    rows = sums_ref.shape[0]
    back = dot(score_ref[...], router_ref[...], ((0,), (0,)))
    column = jnp.sum(column_ref[...], axis=0, keepdims=True)
    high = column.astype(BF16)
    low = (column - high.astype(F32)).astype(BF16)
    mask = fits(rows, capacity, per_row)
    high, low = [
        dot(jnp.where(mask, part.astype(F32), 0.0).astype(BF16), fold_ref[...]) for part in (high, low)
    ]
    sums = sums_ref[...].astype(F32)
    out_ref[:, :LANES] = (sums[:, :LANES] + back + high).astype(BF16)
    out_ref[:, LANES:] = (sums[:, LANES:] + low).astype(BF16)


def combine_kernel(
    capacity, per_row, got_ref, pick_ref, fold_ref, mixed_ref, token_ref, router_ref
):
    rows = got_ref.shape[0]
    width = mixed_ref.shape[0]
    got = got_ref[...]
    pair = dot(got, pick_ref[...], ((0,), (0,)))
    token_ref[...] = pair[:width].astype(BF16)
    mixed_ref[...] = pair[LANES : LANES + width].astype(BF16)
    spread = [dot(part, fold_ref[...], ((1,), (1,))) for part in (got[:, :LANES], got[:, LANES:])]
    spread = jnp.where(fits(rows, capacity, per_row), spread[0] + spread[1], 0.0)
    columns = jnp.sum(spread.reshape(rows // capacity, capacity, LANES), axis=1)
    router_ref[...] = columns[:, : router_ref.shape[1]]


def shards(tokens, cotangent, routes, router, w_in, w_out):
    tok_count, width = tokens.shape
    experts = router.shape[1]
    sources = lax.axis_size("expert")
    groups = lax.axis_size("dp")
    chips = groups // 2
    capacity = 8
    slots = sources * capacity
    ff = w_in.shape[2]
    lanes = 2 * LANES
    per_row = width // capacity
    same_core = [[2 * chip + core for chip in range(chips)] for core in range(2)]
    swap = [(index, index ^ 1) for index in range(groups)]
    dp = lax.axis_index("dp")
    at = jnp.stack([lax.axis_index("expert"), dp % 2]).astype(jnp.int32)
    fold = np.zeros((LANES, LANES), np.float32)
    for lane in range(width):
        fold[lane, width + lane % per_row] = 1
    fold = jnp.asarray(fold, BF16)

    whole_block = lambda i: (0, 0)
    mine, pick = pl.pallas_call(
        functools.partial(place_kernel, capacity, experts),
        grid=(1,),
        in_specs=[
            pl.BlockSpec((2, tok_count), whole_block),
            pl.BlockSpec((width, tok_count), whole_block),
            pl.BlockSpec((width, tok_count), whole_block),
        ],
        out_specs=[
            pl.BlockSpec((slots, lanes), whole_block),
            pl.BlockSpec((slots, tok_count), whole_block),
        ],
        out_shape=(
            jax.ShapeDtypeStruct((slots, lanes), BF16),
            jax.ShapeDtypeStruct((slots, tok_count), BF16),
        ),
        compiler_params=pltpu.CompilerParams(vmem_limit_bytes=60 * 1024 * 1024),
        cost_estimate=pl.CostEstimate(
            flops=60_000_000, bytes_accessed=500_000, transcendentals=0
        ),
    )(routes.T, tokens.T, cotangent.T)
    got = lax.all_to_all(
        mine.reshape(sources, capacity, lanes), "expert", split_axis=0, concat_axis=0, tiled=True
    ).reshape(slots, lanes)

    got, w_in, w_out, router = lax.optimization_barrier((got, w_in, w_out, router))
    whole = lax.all_gather(got[None], "dp", axis=0, tiled=True)

    spare = LANES - width
    front = jnp.pad(w_in[0].reshape(groups, width, ff), ((0, 0), (0, spare), (0, 0)))
    front = front.reshape(groups * LANES, ff)
    back = jnp.pad(w_out[0].reshape(ff, groups, width), ((0, 0), (0, 0), (0, spare)))
    back = back.reshape(ff, groups * LANES)
    scorer = jnp.pad(
        router.T.reshape(experts, groups, width), ((0, LANES - experts), (0, 0), (0, spare))
    ).reshape(LANES, groups * LANES)

    send, pre, hidden, gating, gate_term, chances = pl.pallas_call(
        functools.partial(expert_kernel, experts),
        in_specs=[SMEM, pl.BlockSpec(memory_space=pltpu.HBM), VMEM, VMEM, VMEM],
        out_specs=[VMEM] * 6,
        scratch_shapes=[
            pltpu.VMEM((groups, slots, lanes), BF16),
            pltpu.VMEM((slots, ff), F32),
            pltpu.VMEM((slots, ff), F32),
            pltpu.VMEM((slots, LANES), F32),
            pltpu.SemaphoreType.DMA((4,)),
        ],
        out_shape=(
            jax.ShapeDtypeStruct((chips, slots, lanes), BF16),
            jax.ShapeDtypeStruct((slots, ff), BF16),
            jax.ShapeDtypeStruct((slots, ff), BF16),
            jax.ShapeDtypeStruct((slots, LANES), F32),
            jax.ShapeDtypeStruct((8, slots), F32),
            jax.ShapeDtypeStruct((experts, slots), F32),
        ),
        compiler_params=pltpu.CompilerParams(vmem_limit_bytes=44 * 1024 * 1024),
        cost_estimate=pl.CostEstimate(
            flops=4_000_000_000, bytes_accessed=16_000_000, transcendentals=slots * ff
        ),
    )(at, whole, front, back, scorer)

    swapped = lax.ppermute(send, "dp", swap)
    keep = call(
        keep_kernel,
        jax.ShapeDtypeStruct((chips, slots, lanes), BF16),
        [SMEM] + [VMEM] * 5,
        flops=2_000_000_000,
        moved=8_000_000,
    )(at, pre, hidden, gating, front, back)
    halves = keep + swapped
    halves, gate_term = lax.optimization_barrier((halves, gate_term))
    sums = lax.psum_scatter(
        halves, "dp", scatter_dimension=0, axis_index_groups=same_core, tiled=True
    )

    gates = lax.all_to_all(
        jnp.broadcast_to(gate_term[None, :1], (groups, 1, slots)),
        "dp",
        split_axis=0,
        concat_axis=0,
        tiled=True,
    ).reshape(groups, slots)
    score_grad, router_part = call(
        router_kernel,
        (
            jax.ShapeDtypeStruct((experts, slots), BF16),
            jax.ShapeDtypeStruct((experts, LANES), F32),
        ),
        [SMEM] + [VMEM] * 3,
    )(at, gates, chances, got)
    router_column = lax.all_to_all(
        router_part.reshape(experts, 1, LANES), "expert", split_axis=0, concat_axis=0, tiled=True
    ).reshape(experts, LANES)

    router_slice = lax.dynamic_slice_in_dim(router.T, dp * width, width, 1)
    router_slice = jnp.pad(router_slice, ((0, 0), (0, spare)))
    home = call(
        functools.partial(return_kernel, capacity, per_row),
        jax.ShapeDtypeStruct((slots, lanes), BF16),
        [VMEM] * 5,
    )(sums.reshape(slots, lanes), score_grad, router_slice, router_column, fold)
    home = lax.all_to_all(
        home.reshape(sources, capacity, lanes), "expert", split_axis=0, concat_axis=0, tiled=True
    ).reshape(slots, lanes)
    mixed, token_grad, router_grad = call(
        functools.partial(combine_kernel, capacity, per_row),
        (
            jax.ShapeDtypeStruct((width, tok_count), BF16),
            jax.ShapeDtypeStruct((width, tok_count), BF16),
            jax.ShapeDtypeStruct((experts, width), F32),
        ),
        [VMEM] * 3,
    )(home, pick, fold)
    return (mixed.T, token_grad.T, router_grad.T)


def solution(mesh):
    placed = (
        P("expert", "dp"),
        P("expert", "dp"),
        P("expert", None),
        P(),
        P("expert", None, "dp"),
        P("expert", "dp", None),
    )
    return jax.shard_map(
        shards,
        mesh=mesh,
        in_specs=placed,
        out_specs=(P("expert", "dp"), P("expert", "dp"), P("dp", None)),
        check_vma=False,
    )
```

```python
import functools

import jax
import jax.numpy as jnp
import numpy as np
from jax import lax
from jax.experimental import pallas as pl
from jax.experimental.pallas import tpu as pltpu
from jax.sharding import PartitionSpec as P

F32 = jnp.float32
BF16 = jnp.bfloat16
LANES = 128
VMEM_LIMIT = 24 * 1024 * 1024
VMEM = pl.BlockSpec(memory_space=pltpu.VMEM)
HBM = pl.BlockSpec(memory_space=pltpu.HBM)
SMEM = pl.BlockSpec(memory_space=pltpu.SMEM)


def dot(a, b, dims=((1,), (0,))):
    return lax.dot_general(a, b, (dims, ((), ())), preferred_element_type=F32)


def call(body, out_shape, in_specs, flops=10_000_000, moved=1_000_000):
    return pl.pallas_call(
        body,
        out_shape=out_shape,
        in_specs=in_specs,
        out_specs=jax.tree.map(lambda _: VMEM, out_shape),
        compiler_params=pltpu.CompilerParams(vmem_limit_bytes=VMEM_LIMIT),
        cost_estimate=pl.CostEstimate(flops=flops, bytes_accessed=moved, transcendentals=0),
    )


def place_kernel(capacity, experts, routes_ref, tok_ref, cot_ref, slots_ref, pick_ref):
    width, rows = tok_ref.shape
    slots = slots_ref.shape[0]
    routes = routes_ref[...]
    number = lax.broadcasted_iota(jnp.int32, (experts, rows), 0)
    hot = [(routes[k : k + 1] == number).astype(F32) for k in range(2)]
    before = lax.broadcasted_iota(jnp.int32, (rows, rows), 0) < lax.broadcasted_iota(
        jnp.int32, (rows, rows), 1
    )
    before = before.astype(F32).astype(BF16)
    first = dot(hot[0].astype(BF16), before)
    second = dot(hot[1].astype(BF16), before) + jnp.sum(hot[0], axis=1, keepdims=True)
    rank = [
        jnp.sum(first * hot[0], axis=0, keepdims=True),
        jnp.sum(second * hot[1], axis=0, keepdims=True),
    ]
    place = lax.broadcasted_iota(jnp.int32, (slots, rows), 0)
    target = [routes[k : k + 1] * capacity + rank[k].astype(jnp.int32) for k in range(2)]
    pick = ((place == target[0]) | (place == target[1])).astype(F32).astype(BF16)
    pick_ref[...] = pick
    blank = jnp.zeros((slots, LANES - width), BF16)
    for at, ref in ((0, tok_ref), (LANES, cot_ref)):
        slots_ref[:, at : at + width] = dot(pick, ref[...], ((1,), (1,))).astype(BF16)
        slots_ref[:, at + width : at + LANES] = blank


def terms(at, rows, pre, hidden, gating, front_ref, back_ref, out_ref):
    chips = out_ref.shape[0]
    for pair in range(chips // 2):
        offsets = [
            pl.multiple_of((2 * (2 * pair + j) + at) * LANES, LANES) for j in range(2)
        ]
        front = jnp.concatenate([front_ref[pl.ds(o, LANES), :] for o in offsets], axis=0)
        back = jnp.concatenate([back_ref[:, pl.ds(o, LANES)] for o in offsets], axis=1)
        grad = dot(pre, front, ((1,), (1,)))
        out = dot(hidden, back)
        for j in range(2):
            lanes = slice(j * LANES, (j + 1) * LANES)
            out_ref[2 * pair + j, rows, :LANES] = grad[:, lanes].astype(BF16)
            out_ref[2 * pair + j, rows, LANES:] = (gating * out[:, lanes]).astype(BF16)


def expert_kernel(
    experts,
    at_ref,
    whole_ref,
    front_ref,
    back_ref,
    router_ref,
    send_ref,
    pre_ref,
    hidden_ref,
    gating_ref,
    gate_ref,
    chance_ref,
    got,
    wide,
    sems,
):
    parts = sems.shape[0] - 1
    groups, slots = got.shape[0], got.shape[1]
    chunk = slots // parts
    own = at_ref[0]
    copies = []
    for i in range(parts):
        rows = pl.ds(i * chunk, chunk)
        copies.append(pltpu.make_async_copy(whole_ref.at[:, rows], got.at[:, rows], sems.at[i]))
    wide_copy = pltpu.make_async_copy(back_ref, wide, sems.at[parts])
    copies[0].start()
    wide_copy.start()
    for copy in copies[1:]:
        copy.start()
    for i in range(parts):
        copies[i].wait()
        rows = slice(i * chunk, (i + 1) * chunk)
        tok = jnp.concatenate([got[j, rows, :LANES] for j in range(groups)], axis=1)
        cot = jnp.concatenate([got[j, rows, LANES:] for j in range(groups)], axis=1)
        x = dot(tok, front_ref[...])
        scores = dot(tok, router_ref[...], ((1,), (1,)))
        if i == 0:
            wide_copy.wait()
        up = dot(cot, wide[...], ((1,), (1,)))
        lane = lax.broadcasted_iota(jnp.int32, scores.shape, 1)
        scores = jnp.where(lane < experts, scores, -jnp.inf)
        top = jnp.max(scores, axis=1, keepdims=True)
        raised = jnp.exp(scores - top)
        chances = raised / jnp.sum(raised, axis=1, keepdims=True)
        gating = jnp.sum(jnp.where(lane == own, chances, 0.0), axis=1, keepdims=True)
        c = np.float32(np.sqrt(2.0 / np.pi))
        square = x * x
        t = jnp.tanh(c * (x + 0.044715 * (square * x)))
        half = 0.5 * (1.0 + t)
        hidden = (x * half).astype(BF16)
        slope = half + 0.5 * x * (1.0 - t * t) * (c * (1.0 + 3 * 0.044715 * square))
        pre_ref[rows, :] = (slope * (gating * up)).astype(BF16)
        hidden_ref[rows, :] = hidden
        gate = jnp.sum(hidden.astype(F32) * up, axis=1, keepdims=True)
        gating_ref[rows, :] = jnp.broadcast_to(gating, (chunk, LANES))
        turned = jnp.where(lane == experts, gate, chances).T
        chance_ref[:, rows] = turned[:experts]
        gate_ref[:, rows] = turned[experts : experts + 8]
        terms(
            1 - at_ref[1],
            rows,
            pre_ref[rows, :],
            hidden_ref[rows, :],
            gating_ref[rows, :],
            front_ref,
            wide,
            send_ref,
        )


def keep_kernel(at_ref, pre_ref, hidden_ref, gating_ref, front_ref, back_ref, keep_ref):
    terms(
        at_ref[1],
        slice(None),
        pre_ref[...],
        hidden_ref[...],
        gating_ref[...],
        front_ref,
        back_ref,
        keep_ref,
    )


def router_kernel(at_ref, gates_ref, chance_ref, slots_ref, score_ref, part_ref):
    gate = jnp.sum(gates_ref[...], axis=0, keepdims=True)
    chances = chance_ref[...]
    own = (lax.broadcasted_iota(jnp.int32, chances.shape, 0) == at_ref[0]).astype(F32)
    gating = jnp.sum(chances * own, axis=0, keepdims=True)
    score = ((gate * gating) * (own - chances)).astype(BF16)
    score_ref[...] = score
    part_ref[...] = dot(score, slots_ref[:, :LANES])


def fits(rows, capacity, per_row):
    row = lax.broadcasted_iota(jnp.int32, (rows, LANES), 0) & (capacity - 1)
    lane = lax.broadcasted_iota(jnp.int32, (rows, LANES), 1)
    return (lane >= row * per_row) & (lane < row * per_row + per_row)


def return_kernel(
    capacity, per_row, sums_ref, score_ref, router_ref, column_ref, fold_ref, out_ref
):
    rows = sums_ref.shape[0]
    back = dot(score_ref[...], router_ref[...], ((0,), (0,)))
    column = jnp.sum(column_ref[...], axis=0, keepdims=True)
    high = column.astype(BF16)
    low = (column - high.astype(F32)).astype(BF16)
    mask = fits(rows, capacity, per_row)
    high, low = [
        dot(jnp.where(mask, part.astype(F32), 0.0).astype(BF16), fold_ref[...]) for part in (high, low)
    ]
    sums = sums_ref[...].astype(F32)
    out_ref[:, :LANES] = (sums[:, :LANES] + back + high).astype(BF16)
    out_ref[:, LANES:] = (sums[:, LANES:] + low).astype(BF16)


def combine_kernel(
    capacity, per_row, got_ref, pick_ref, fold_ref, mixed_ref, token_ref, router_ref
):
    rows = got_ref.shape[0]
    width = mixed_ref.shape[0]
    got = got_ref[...]
    pair = dot(got, pick_ref[...], ((0,), (0,)))
    token_ref[...] = pair[:width].astype(BF16)
    mixed_ref[...] = pair[LANES : LANES + width].astype(BF16)
    spread = [dot(part, fold_ref[...], ((1,), (1,))) for part in (got[:, :LANES], got[:, LANES:])]
    spread = jnp.where(fits(rows, capacity, per_row), spread[0] + spread[1], 0.0)
    columns = jnp.sum(spread.reshape(rows // capacity, capacity, LANES), axis=1)
    router_ref[...] = columns[:, : router_ref.shape[1]]


def shards(tokens, cotangent, routes, router, w_in, w_out):
    tok_count, width = tokens.shape
    experts = router.shape[1]
    sources = lax.axis_size("expert")
    groups = lax.axis_size("dp")
    chips = groups // 2
    capacity = 8
    slots = sources * capacity
    ff = w_in.shape[2]
    lanes = 2 * LANES
    per_row = width // capacity
    same_core = [[2 * chip + core for chip in range(chips)] for core in range(2)]
    swap = [(index, index ^ 1) for index in range(groups)]
    dp = lax.axis_index("dp")
    at = jnp.stack([lax.axis_index("expert"), dp % 2]).astype(jnp.int32)
    fold = np.zeros((LANES, LANES), np.float32)
    for lane in range(width):
        fold[lane, width + lane % per_row] = 1
    fold = jnp.asarray(fold, BF16)

    whole_block = lambda i: (0, 0)
    mine, pick = pl.pallas_call(
        functools.partial(place_kernel, capacity, experts),
        grid=(1,),
        in_specs=[
            pl.BlockSpec((2, tok_count), whole_block),
            pl.BlockSpec((width, tok_count), whole_block),
            pl.BlockSpec((width, tok_count), whole_block),
        ],
        out_specs=[
            pl.BlockSpec((slots, lanes), whole_block),
            pl.BlockSpec((slots, tok_count), whole_block),
        ],
        out_shape=(
            jax.ShapeDtypeStruct((slots, lanes), BF16),
            jax.ShapeDtypeStruct((slots, tok_count), BF16),
        ),
        compiler_params=pltpu.CompilerParams(vmem_limit_bytes=60 * 1024 * 1024),
        cost_estimate=pl.CostEstimate(
            flops=60_000_000, bytes_accessed=500_000, transcendentals=0
        ),
    )(routes.T, tokens.T, cotangent.T)
    got = lax.all_to_all(
        mine.reshape(sources, capacity, lanes), "expert", split_axis=0, concat_axis=0, tiled=True
    ).reshape(slots, lanes)

    got, w_in, w_out, router = lax.optimization_barrier((got, w_in, w_out, router))
    whole = lax.all_gather(got[None], "dp", axis=0, tiled=True)

    spare = LANES - width
    front = jnp.pad(w_in[0].reshape(groups, width, ff), ((0, 0), (0, spare), (0, 0)))
    front = front.reshape(groups * LANES, ff)
    back = jnp.pad(w_out[0].reshape(ff, groups, width), ((0, 0), (0, 0), (0, spare)))
    back = back.reshape(ff, groups * LANES)
    scorer = jnp.pad(
        router.T.reshape(experts, groups, width), ((0, LANES - experts), (0, 0), (0, spare))
    ).reshape(LANES, groups * LANES)

    send, pre, hidden, gating, gate_term, chances = pl.pallas_call(
        functools.partial(expert_kernel, experts),
        in_specs=[SMEM, HBM, VMEM, HBM, VMEM],
        out_specs=[VMEM] * 6,
        scratch_shapes=[
            pltpu.VMEM((groups, slots, lanes), BF16),
            pltpu.VMEM((ff, groups * LANES), BF16),
            pltpu.SemaphoreType.DMA((3,)),
        ],
        out_shape=(
            jax.ShapeDtypeStruct((chips, slots, lanes), BF16),
            jax.ShapeDtypeStruct((slots, ff), BF16),
            jax.ShapeDtypeStruct((slots, ff), BF16),
            jax.ShapeDtypeStruct((slots, LANES), F32),
            jax.ShapeDtypeStruct((8, slots), F32),
            jax.ShapeDtypeStruct((experts, slots), F32),
        ),
        compiler_params=pltpu.CompilerParams(vmem_limit_bytes=47 * 1024 * 1024),
        cost_estimate=pl.CostEstimate(
            flops=4_000_000_000, bytes_accessed=16_000_000, transcendentals=slots * ff
        ),
    )(at, whole, front, back, scorer)

    swapped = lax.ppermute(send, "dp", swap)
    keep = call(
        keep_kernel,
        jax.ShapeDtypeStruct((chips, slots, lanes), BF16),
        [SMEM] + [VMEM] * 5,
        flops=2_000_000_000,
        moved=8_000_000,
    )(at, pre, hidden, gating, front, back)
    halves = keep + swapped
    halves, gate_term = lax.optimization_barrier((halves, gate_term))
    sums = lax.psum_scatter(
        halves, "dp", scatter_dimension=0, axis_index_groups=same_core, tiled=True
    )

    gates = lax.all_to_all(
        jnp.broadcast_to(gate_term[None, :1], (groups, 1, slots)),
        "dp",
        split_axis=0,
        concat_axis=0,
        tiled=True,
    ).reshape(groups, slots)
    score_grad, router_part = call(
        router_kernel,
        (
            jax.ShapeDtypeStruct((experts, slots), BF16),
            jax.ShapeDtypeStruct((experts, LANES), F32),
        ),
        [SMEM] + [VMEM] * 3,
    )(at, gates, chances, got)
    router_column = lax.all_to_all(
        router_part.reshape(experts, 1, LANES), "expert", split_axis=0, concat_axis=0, tiled=True
    ).reshape(experts, LANES)

    router_slice = lax.dynamic_slice_in_dim(router.T, dp * width, width, 1)
    router_slice = jnp.pad(router_slice, ((0, 0), (0, spare)))
    home = call(
        functools.partial(return_kernel, capacity, per_row),
        jax.ShapeDtypeStruct((slots, lanes), BF16),
        [VMEM] * 5,
    )(sums.reshape(slots, lanes), score_grad, router_slice, router_column, fold)
    home = lax.all_to_all(
        home.reshape(sources, capacity, lanes), "expert", split_axis=0, concat_axis=0, tiled=True
    ).reshape(slots, lanes)
    mixed, token_grad, router_grad = call(
        functools.partial(combine_kernel, capacity, per_row),
        (
            jax.ShapeDtypeStruct((width, tok_count), BF16),
            jax.ShapeDtypeStruct((width, tok_count), BF16),
            jax.ShapeDtypeStruct((experts, width), F32),
        ),
        [VMEM] * 3,
    )(home, pick, fold)
    return (mixed.T, token_grad.T, router_grad.T)


def solution(mesh):
    placed = (
        P("expert", "dp"),
        P("expert", "dp"),
        P("expert", None),
        P(),
        P("expert", None, "dp"),
        P("expert", "dp", None),
    )
    return jax.shard_map(
        shards,
        mesh=mesh,
        in_specs=placed,
        out_specs=(P("expert", "dp"), P("expert", "dp"), P("dp", None)),
        check_vma=False,
    )
```

```python
import functools

import jax
import jax.numpy as jnp
import numpy as np
from jax import lax
from jax.experimental import pallas as pl
from jax.experimental.pallas import tpu as pltpu
from jax.sharding import PartitionSpec as P

F32 = jnp.float32
BF16 = jnp.bfloat16
LANES = 128
EXPERT_VMEM = 42 * 1024 * 1024
VMEM_LIMIT = 24 * 1024 * 1024
VMEM = pl.BlockSpec(memory_space=pltpu.VMEM)
HBM = pl.BlockSpec(memory_space=pltpu.HBM)
SMEM = pl.BlockSpec(memory_space=pltpu.SMEM)


def dot(a, b, dims=((1,), (0,))):
    return lax.dot_general(a, b, (dims, ((), ())), preferred_element_type=F32)


def call(body, out_shape, in_specs, flops=10_000_000, moved=1_000_000):
    return pl.pallas_call(
        body,
        out_shape=out_shape,
        in_specs=in_specs,
        out_specs=jax.tree.map(lambda _: VMEM, out_shape),
        compiler_params=pltpu.CompilerParams(vmem_limit_bytes=VMEM_LIMIT),
        cost_estimate=pl.CostEstimate(flops=flops, bytes_accessed=moved, transcendentals=0),
    )


def place_kernel(capacity, experts, routes_ref, tok_ref, cot_ref, slots_ref, pick_ref):
    width, rows = tok_ref.shape
    slots = slots_ref.shape[0]
    routes = routes_ref[...]
    number = lax.broadcasted_iota(jnp.int32, (experts, rows), 0)
    hot = [(routes[k : k + 1] == number).astype(F32) for k in range(2)]
    before = lax.broadcasted_iota(jnp.int32, (rows, rows), 0) < lax.broadcasted_iota(
        jnp.int32, (rows, rows), 1
    )
    before = before.astype(F32).astype(BF16)
    first = dot(hot[0].astype(BF16), before)
    second = dot(hot[1].astype(BF16), before) + jnp.sum(hot[0], axis=1, keepdims=True)
    rank = [
        jnp.sum(first * hot[0], axis=0, keepdims=True),
        jnp.sum(second * hot[1], axis=0, keepdims=True),
    ]
    place = lax.broadcasted_iota(jnp.int32, (slots, rows), 0)
    target = [routes[k : k + 1] * capacity + rank[k].astype(jnp.int32) for k in range(2)]
    pick = ((place == target[0]) | (place == target[1])).astype(F32).astype(BF16)
    pick_ref[...] = pick
    blank = jnp.zeros((slots, LANES - width), BF16)
    for at, ref in ((0, tok_ref), (LANES, cot_ref)):
        slots_ref[:, at : at + width] = dot(pick, ref[...], ((1,), (1,))).astype(BF16)
        slots_ref[:, at + width : at + LANES] = blank


def terms(both_ref, gating_ref, own_ref, pair):
    rows = slice(pair * 2 * LANES, (pair + 1) * 2 * LANES)
    grad = dot(both_ref[0], own_ref[0, rows, :], ((1,), (1,)))
    out = dot(both_ref[1], own_ref[1, rows, :], ((1,), (1,)))
    for j in range(2):
        lanes = slice(j * LANES, (j + 1) * LANES)
        yield j, grad[:, lanes], gating_ref[...] * out[:, lanes]


def expert_kernel(
    experts,
    at_ref,
    whole_ref,
    front_ref,
    back_ref,
    router_ref,
    both_ref,
    gating_ref,
    gate_ref,
    chance_ref,
    got,
    wide,
    sems,
):
    parts = sems.shape[0] - 1
    groups, slots = got.shape[0], got.shape[1]
    chunk = slots // parts
    own = at_ref[0]
    copies = []
    for i in range(parts):
        rows = pl.ds(i * chunk, chunk)
        copies.append(pltpu.make_async_copy(whole_ref.at[:, rows], got.at[:, rows], sems.at[i]))
    wide_copy = pltpu.make_async_copy(back_ref, wide, sems.at[parts])
    copies[0].start()
    wide_copy.start()
    for copy in copies[1:]:
        copy.start()
    for i in range(parts):
        copies[i].wait()
        rows = slice(i * chunk, (i + 1) * chunk)
        tok = jnp.concatenate([got[j, rows, :LANES] for j in range(groups)], axis=1)
        cot = jnp.concatenate([got[j, rows, LANES:] for j in range(groups)], axis=1)
        x = dot(tok, front_ref[...])
        scores = dot(tok, router_ref[...], ((1,), (1,)))
        if i == 0:
            wide_copy.wait()
        up = dot(cot, wide[...])
        lane = lax.broadcasted_iota(jnp.int32, scores.shape, 1)
        scores = jnp.where(lane < experts, scores, -jnp.inf)
        top = jnp.max(scores, axis=1, keepdims=True)
        raised = jnp.exp(scores - top)
        chances = raised / jnp.sum(raised, axis=1, keepdims=True)
        gating = jnp.sum(jnp.where(lane == own, chances, 0.0), axis=1, keepdims=True)
        c = np.float32(np.sqrt(2.0 / np.pi))
        square = x * x
        t = jnp.tanh(c * (x + 0.044715 * (square * x)))
        half = 0.5 * (1.0 + t)
        hidden = (x * half).astype(BF16)
        slope = half + 0.5 * x * (1.0 - t * t) * (c * (1.0 + 3 * 0.044715 * square))
        both_ref[0, rows, :] = (slope * (gating * up)).astype(BF16)
        both_ref[1, rows, :] = hidden
        gate = jnp.sum(hidden.astype(F32) * up, axis=1, keepdims=True)
        gating_ref[rows, :] = jnp.broadcast_to(gating, (chunk, LANES))
        turned = jnp.where(lane == experts, gate, chances).T
        chance_ref[:, rows] = turned[:experts]
        gate_ref[:, rows] = turned[experts : experts + 8]


def keep_kernel(both_ref, gating_ref, own_ref, keep_ref):
    for pair in range(keep_ref.shape[0] // 2):
        for j, grad, out in terms(both_ref, gating_ref, own_ref, pair):
            keep_ref[2 * pair + j, :, :LANES] = grad.astype(BF16)
            keep_ref[2 * pair + j, :, LANES:] = out.astype(BF16)


def other_kernel(both_ref, gating_ref, own_ref, keep_ref, sum_ref):
    pair = pl.program_id(0)
    for j, grad, out in terms(both_ref, gating_ref, own_ref, 0):
        kept = keep_ref[2 * pair + j].astype(F32)
        sum_ref[j, :, :LANES] = (grad + kept[:, :LANES]).astype(BF16)
        sum_ref[j, :, LANES:] = (out + kept[:, LANES:]).astype(BF16)


def router_kernel(at_ref, gates_ref, chance_ref, slots_ref, score_ref, part_ref):
    gate = jnp.sum(gates_ref[...], axis=0, keepdims=True)
    chances = chance_ref[...]
    own = (lax.broadcasted_iota(jnp.int32, chances.shape, 0) == at_ref[0]).astype(F32)
    gating = jnp.sum(chances * own, axis=0, keepdims=True)
    score = ((gate * gating) * (own - chances)).astype(BF16)
    score_ref[...] = score
    part_ref[...] = dot(score, slots_ref[:, :LANES])


def fits(rows, capacity, per_row):
    row = lax.broadcasted_iota(jnp.int32, (rows, LANES), 0) & (capacity - 1)
    lane = lax.broadcasted_iota(jnp.int32, (rows, LANES), 1)
    return (lane >= row * per_row) & (lane < row * per_row + per_row)


def return_kernel(
    capacity, per_row, sums_ref, score_ref, router_ref, column_ref, fold_ref, out_ref
):
    rows = sums_ref.shape[0]
    back = dot(score_ref[...], router_ref[...], ((0,), (0,)))
    column = jnp.sum(column_ref[...], axis=0, keepdims=True)
    high = column.astype(BF16)
    low = (column - high.astype(F32)).astype(BF16)
    mask = fits(rows, capacity, per_row)
    high, low = [
        dot(jnp.where(mask, part.astype(F32), 0.0).astype(BF16), fold_ref[...]) for part in (high, low)
    ]
    sums = sums_ref[...].astype(F32)
    out_ref[:, :LANES] = (sums[:, :LANES] + back + high).astype(BF16)
    out_ref[:, LANES:] = (sums[:, LANES:] + low).astype(BF16)


def combine_kernel(
    capacity, per_row, got_ref, pick_ref, fold_ref, mixed_ref, token_ref, router_ref
):
    rows = got_ref.shape[0]
    width = mixed_ref.shape[0]
    got = got_ref[...]
    pair = dot(got, pick_ref[...], ((0,), (0,)))
    token_ref[...] = pair[:width].astype(BF16)
    mixed_ref[...] = pair[LANES : LANES + width].astype(BF16)
    spread = [dot(part, fold_ref[...], ((1,), (1,))) for part in (got[:, :LANES], got[:, LANES:])]
    spread = jnp.where(fits(rows, capacity, per_row), spread[0] + spread[1], 0.0)
    columns = jnp.sum(spread.reshape(rows // capacity, capacity, LANES), axis=1)
    router_ref[...] = columns[:, : router_ref.shape[1]]


def shards(tokens, cotangent, routes, router, w_in, w_out):
    tok_count, width = tokens.shape
    experts = router.shape[1]
    sources = lax.axis_size("expert")
    groups = lax.axis_size("dp")
    chips = groups // 2
    capacity = 8
    slots = sources * capacity
    ff = w_in.shape[2]
    lanes = 2 * LANES
    per_row = width // capacity
    same_core = [[2 * chip + core for chip in range(chips)] for core in range(2)]
    swap = [(index, index ^ 1) for index in range(groups)]
    dp = lax.axis_index("dp")
    at = lax.axis_index("expert").astype(jnp.int32)[None]
    fold = np.zeros((LANES, LANES), np.float32)
    for lane in range(width):
        fold[lane, width + lane % per_row] = 1
    fold = jnp.asarray(fold, BF16)

    whole_block = lambda i: (0, 0)
    mine, pick = pl.pallas_call(
        functools.partial(place_kernel, capacity, experts),
        grid=(1,),
        in_specs=[
            pl.BlockSpec((2, tok_count), whole_block),
            pl.BlockSpec((width, tok_count), whole_block),
            pl.BlockSpec((width, tok_count), whole_block),
        ],
        out_specs=[
            pl.BlockSpec((slots, lanes), whole_block),
            pl.BlockSpec((slots, tok_count), whole_block),
        ],
        out_shape=(
            jax.ShapeDtypeStruct((slots, lanes), BF16),
            jax.ShapeDtypeStruct((slots, tok_count), BF16),
        ),
        compiler_params=pltpu.CompilerParams(vmem_limit_bytes=60 * 1024 * 1024),
        cost_estimate=pl.CostEstimate(
            flops=60_000_000, bytes_accessed=500_000, transcendentals=0
        ),
    )(routes.T, tokens.T, cotangent.T)
    got = lax.all_to_all(
        mine.reshape(sources, capacity, lanes), "expert", split_axis=0, concat_axis=0, tiled=True
    ).reshape(slots, lanes)

    got, w_in, w_out, router = lax.optimization_barrier((got, w_in, w_out, router))
    whole = lax.all_gather(got[None], "dp", axis=0, tiled=True)

    spare = LANES - width
    front = jnp.pad(w_in[0].reshape(groups, width, ff), ((0, 0), (0, spare), (0, 0)))
    front = front.reshape(groups * LANES, ff)
    back = jnp.pad(w_out[0].T.reshape(groups, width, ff), ((0, 0), (0, spare), (0, 0)))
    back = back.reshape(groups * LANES, ff)
    core = dp % 2

    def half(which):
        picked = [
            lax.dynamic_index_in_dim(part.reshape(chips, 2, LANES, ff), which, 1, keepdims=False)
            for part in (front, back)
        ]
        return jnp.stack(picked).reshape(2, chips * LANES, ff)

    own = half(core)
    other = lax.ppermute(half(1 - core), "dp", swap)
    scorer = jnp.pad(
        router.T.reshape(experts, groups, width), ((0, LANES - experts), (0, 0), (0, spare))
    ).reshape(LANES, groups * LANES)

    whole, other, own = lax.optimization_barrier((whole, other, own))
    both, gating, gate_term, chances = pl.pallas_call(
        functools.partial(expert_kernel, experts),
        in_specs=[SMEM, HBM, VMEM, HBM, VMEM],
        out_specs=[VMEM] * 4,
        scratch_shapes=[
            pltpu.VMEM((groups, slots, lanes), BF16),
            pltpu.VMEM((groups * LANES, ff), BF16),
            pltpu.SemaphoreType.DMA((3,)),
        ],
        out_shape=(
            jax.ShapeDtypeStruct((2, slots, ff), BF16),
            jax.ShapeDtypeStruct((slots, LANES), F32),
            jax.ShapeDtypeStruct((8, slots), F32),
            jax.ShapeDtypeStruct((experts, slots), F32),
        ),
        compiler_params=pltpu.CompilerParams(vmem_limit_bytes=EXPERT_VMEM),
        cost_estimate=pl.CostEstimate(
            flops=3_000_000_000, bytes_accessed=16_000_000, transcendentals=slots * ff
        ),
    )(at, whole, front, back, scorer)

    both_other = lax.ppermute(both, "dp", swap)
    keep = call(
        keep_kernel,
        jax.ShapeDtypeStruct((chips, slots, lanes), BF16),
        [VMEM] * 3,
        flops=2_000_000_000,
        moved=8_000_000,
    )(both, gating, own)
    halves = pl.pallas_call(
        other_kernel,
        grid=(chips // 2,),
        in_specs=[VMEM, VMEM, pl.BlockSpec((2, 2 * LANES, ff), lambda i: (0, i, 0)), VMEM],
        out_specs=pl.BlockSpec((2, slots, lanes), lambda i: (i, 0, 0)),
        out_shape=jax.ShapeDtypeStruct((chips, slots, lanes), BF16),
        compiler_params=pltpu.CompilerParams(vmem_limit_bytes=VMEM_LIMIT),
        cost_estimate=pl.CostEstimate(
            flops=2_000_000_000, bytes_accessed=8_000_000, transcendentals=0
        ),
    )(both_other, gating, other, keep)
    halves, gate_term = lax.optimization_barrier((halves, gate_term))
    sums = lax.psum_scatter(
        halves, "dp", scatter_dimension=0, axis_index_groups=same_core, tiled=True
    )

    gates = lax.all_to_all(
        jnp.broadcast_to(gate_term[None, :1], (groups, 1, slots)),
        "dp",
        split_axis=0,
        concat_axis=0,
        tiled=True,
    ).reshape(groups, slots)
    score_grad, router_part = call(
        router_kernel,
        (
            jax.ShapeDtypeStruct((experts, slots), BF16),
            jax.ShapeDtypeStruct((experts, LANES), F32),
        ),
        [SMEM] + [VMEM] * 3,
    )(at, gates, chances, got)
    router_column = lax.all_to_all(
        router_part.reshape(experts, 1, LANES), "expert", split_axis=0, concat_axis=0, tiled=True
    ).reshape(experts, LANES)

    router_slice = lax.dynamic_slice_in_dim(router.T, dp * width, width, 1)
    router_slice = jnp.pad(router_slice, ((0, 0), (0, spare)))
    home = call(
        functools.partial(return_kernel, capacity, per_row),
        jax.ShapeDtypeStruct((slots, lanes), BF16),
        [VMEM] * 5,
    )(sums.reshape(slots, lanes), score_grad, router_slice, router_column, fold)
    home = lax.all_to_all(
        home.reshape(sources, capacity, lanes), "expert", split_axis=0, concat_axis=0, tiled=True
    ).reshape(slots, lanes)
    mixed, token_grad, router_grad = call(
        functools.partial(combine_kernel, capacity, per_row),
        (
            jax.ShapeDtypeStruct((width, tok_count), BF16),
            jax.ShapeDtypeStruct((width, tok_count), BF16),
            jax.ShapeDtypeStruct((experts, width), F32),
        ),
        [VMEM] * 3,
    )(home, pick, fold)
    return (mixed.T, token_grad.T, router_grad.T)


def solution(mesh):
    placed = (
        P("expert", "dp"),
        P("expert", "dp"),
        P("expert", None),
        P(),
        P("expert", None, "dp"),
        P("expert", "dp", None),
    )
    return jax.shard_map(
        shards,
        mesh=mesh,
        in_specs=placed,
        out_specs=(P("expert", "dp"), P("expert", "dp"), P("dp", None)),
        check_vma=False,
    )
```

```python
import functools

import jax
import jax.numpy as jnp
import numpy as np
from jax import lax
from jax.experimental import pallas as pl
from jax.experimental.pallas import tpu as pltpu
from jax.sharding import PartitionSpec as P

F32 = jnp.float32
BF16 = jnp.bfloat16
LANES = 128
EXPERT_VMEM = 49 * 1024 * 1024
VMEM_LIMIT = 24 * 1024 * 1024
VMEM = pl.BlockSpec(memory_space=pltpu.VMEM)
HBM = pl.BlockSpec(memory_space=pltpu.HBM)
SMEM = pl.BlockSpec(memory_space=pltpu.SMEM)


def dot(a, b, dims=((1,), (0,))):
    return lax.dot_general(a, b, (dims, ((), ())), preferred_element_type=F32)


def call(body, out_shape, in_specs, flops=10_000_000, moved=1_000_000):
    return pl.pallas_call(
        body,
        out_shape=out_shape,
        in_specs=in_specs,
        out_specs=jax.tree.map(lambda _: VMEM, out_shape),
        compiler_params=pltpu.CompilerParams(vmem_limit_bytes=VMEM_LIMIT),
        cost_estimate=pl.CostEstimate(flops=flops, bytes_accessed=moved, transcendentals=0),
    )


def place_kernel(capacity, experts, routes_ref, tok_ref, cot_ref, slots_ref, pick_ref):
    width, rows = tok_ref.shape
    slots = slots_ref.shape[0]
    routes = routes_ref[...]
    number = lax.broadcasted_iota(jnp.int32, (experts, rows), 0)
    hot = [(routes[k : k + 1] == number).astype(F32) for k in range(2)]
    before = lax.broadcasted_iota(jnp.int32, (rows, rows), 0) < lax.broadcasted_iota(
        jnp.int32, (rows, rows), 1
    )
    before = before.astype(F32).astype(BF16)
    first = dot(hot[0].astype(BF16), before)
    second = dot(hot[1].astype(BF16), before) + jnp.sum(hot[0], axis=1, keepdims=True)
    rank = [
        jnp.sum(first * hot[0], axis=0, keepdims=True),
        jnp.sum(second * hot[1], axis=0, keepdims=True),
    ]
    place = lax.broadcasted_iota(jnp.int32, (slots, rows), 0)
    target = [routes[k : k + 1] * capacity + rank[k].astype(jnp.int32) for k in range(2)]
    pick = ((place == target[0]) | (place == target[1])).astype(F32).astype(BF16)
    pick_ref[...] = pick
    blank = jnp.zeros((slots, LANES - width), BF16)
    for at, ref in ((0, tok_ref), (LANES, cot_ref)):
        slots_ref[:, at : at + width] = dot(pick, ref[...], ((1,), (1,))).astype(BF16)
        slots_ref[:, at + width : at + LANES] = blank


def terms(both_ref, gating_ref, own_ref, pair):
    rows = pl.ds(pair * 2 * LANES, 2 * LANES)
    grad = dot(both_ref[0], own_ref[0, rows, :], ((1,), (1,)))
    out = dot(both_ref[1], own_ref[1, rows, :], ((1,), (1,)))
    for j in range(2):
        lanes = slice(j * LANES, (j + 1) * LANES)
        yield j, grad[:, lanes], gating_ref[...] * out[:, lanes]


def expert_kernel(
    experts,
    at_ref,
    whole_ref,
    front_ref,
    back_ref,
    router_ref,
    both_ref,
    gating_ref,
    gate_ref,
    chance_ref,
    got,
    deep,
    wide,
    sems,
):
    parts = sems.shape[0] - 2
    groups, slots = got.shape[0], got.shape[1]
    chunk = slots // parts
    own = at_ref[0]
    copies = []
    for i in range(parts):
        rows = pl.ds(i * chunk, chunk)
        copies.append(pltpu.make_async_copy(whole_ref.at[:, rows], got.at[:, rows], sems.at[i]))
    wide_copy = pltpu.make_async_copy(back_ref, wide, sems.at[parts])
    deep_copy = pltpu.make_async_copy(front_ref, deep, sems.at[parts + 1])
    deep_copy.start()
    copies[0].start()
    wide_copy.start()
    for copy in copies[1:]:
        copy.start()
    deep_copy.wait()
    for i in range(parts):
        copies[i].wait()
        rows = slice(i * chunk, (i + 1) * chunk)
        tok = jnp.concatenate([got[j, rows, :LANES] for j in range(groups)], axis=1)
        cot = jnp.concatenate([got[j, rows, LANES:] for j in range(groups)], axis=1)
        x = dot(tok, deep[...])
        scores = dot(tok, router_ref[...], ((1,), (1,)))
        if i == 0:
            wide_copy.wait()
        up = dot(cot, wide[...])
        lane = lax.broadcasted_iota(jnp.int32, scores.shape, 1)
        scores = jnp.where(lane < experts, scores, -jnp.inf)
        top = jnp.max(scores, axis=1, keepdims=True)
        raised = jnp.exp(scores - top)
        chances = raised / jnp.sum(raised, axis=1, keepdims=True)
        gating = jnp.sum(jnp.where(lane == own, chances, 0.0), axis=1, keepdims=True)
        c = np.float32(np.sqrt(2.0 / np.pi))
        square = x * x
        t = jnp.tanh(c * (x + 0.044715 * (square * x)))
        half = 0.5 * (1.0 + t)
        hidden = (x * half).astype(BF16)
        slope = half + 0.5 * x * (1.0 - t * t) * (c * (1.0 + 3 * 0.044715 * square))
        both_ref[0, rows, :] = (slope * (gating * up)).astype(BF16)
        both_ref[1, rows, :] = hidden
        gate = jnp.sum(hidden.astype(F32) * up, axis=1, keepdims=True)
        gating_ref[rows, :] = jnp.broadcast_to(gating, (chunk, LANES))
        turned = jnp.where(lane == experts, gate, chances).T
        chance_ref[:, rows] = turned[:experts]
        gate_ref[:, rows] = turned[experts : experts + 8]


def keep_kernel(both_ref, gating_ref, own_ref, other_ref, keep_ref, near_ref, sem):
    copy = pltpu.make_async_copy(other_ref, near_ref, sem)
    copy.start()
    for pair in range(keep_ref.shape[0] // 2):
        for j, grad, out in terms(both_ref, gating_ref, own_ref, pair):
            keep_ref[2 * pair + j, :, :LANES] = grad.astype(BF16)
            keep_ref[2 * pair + j, :, LANES:] = out.astype(BF16)
    copy.wait()


def other_kernel(both_ref, gating_ref, own_ref, keep_ref, sum_ref, stage, sems):
    copies = []
    for pair in range(keep_ref.shape[0] // 2):
        for j, grad, out in terms(both_ref, gating_ref, own_ref, pair):
            kept = keep_ref[2 * pair + j].astype(F32)
            stage[2 * pair + j, :, :LANES] = (grad + kept[:, :LANES]).astype(BF16)
            stage[2 * pair + j, :, LANES:] = (out + kept[:, LANES:]).astype(BF16)
        two = pl.ds(2 * pair, 2)
        copies.append(pltpu.make_async_copy(stage.at[two], sum_ref.at[two], sems.at[pair]))
        copies[pair].start()
    for copy in copies:
        copy.wait()


def router_kernel(at_ref, gates_ref, chance_ref, slots_ref, score_ref, part_ref):
    gate = jnp.sum(gates_ref[...], axis=0, keepdims=True)
    chances = chance_ref[...]
    own = (lax.broadcasted_iota(jnp.int32, chances.shape, 0) == at_ref[0]).astype(F32)
    gating = jnp.sum(chances * own, axis=0, keepdims=True)
    score = ((gate * gating) * (own - chances)).astype(BF16)
    score_ref[...] = score
    part_ref[...] = dot(score, slots_ref[:, :LANES])


def fits(rows, capacity, per_row):
    row = lax.broadcasted_iota(jnp.int32, (rows, LANES), 0) & (capacity - 1)
    lane = lax.broadcasted_iota(jnp.int32, (rows, LANES), 1)
    return (lane >= row * per_row) & (lane < row * per_row + per_row)


def return_kernel(
    capacity, per_row, sums_ref, score_ref, router_ref, column_ref, fold_ref, out_ref
):
    rows = sums_ref.shape[0]
    back = dot(score_ref[...], router_ref[...], ((0,), (0,)))
    column = jnp.sum(column_ref[...], axis=0, keepdims=True)
    high = column.astype(BF16)
    low = (column - high.astype(F32)).astype(BF16)
    mask = fits(rows, capacity, per_row)
    high, low = [
        dot(jnp.where(mask, part.astype(F32), 0.0).astype(BF16), fold_ref[...]) for part in (high, low)
    ]
    sums = sums_ref[...].astype(F32)
    out_ref[:, :LANES] = (sums[:, :LANES] + back + high).astype(BF16)
    out_ref[:, LANES:] = (sums[:, LANES:] + low).astype(BF16)


def combine_kernel(
    capacity, per_row, got_ref, pick_ref, fold_ref, mixed_ref, token_ref, router_ref
):
    rows = got_ref.shape[0]
    width = mixed_ref.shape[0]
    got = got_ref[...]
    pair = dot(got, pick_ref[...], ((0,), (0,)))
    token_ref[...] = pair[:width].astype(BF16)
    mixed_ref[...] = pair[LANES : LANES + width].astype(BF16)
    spread = [dot(part, fold_ref[...], ((1,), (1,))) for part in (got[:, :LANES], got[:, LANES:])]
    spread = jnp.where(fits(rows, capacity, per_row), spread[0] + spread[1], 0.0)
    columns = jnp.sum(spread.reshape(rows // capacity, capacity, LANES), axis=1)
    router_ref[...] = columns[:, : router_ref.shape[1]]


def shards(tokens, cotangent, routes, router, w_in, w_out):
    tok_count, width = tokens.shape
    experts = router.shape[1]
    sources = lax.axis_size("expert")
    groups = lax.axis_size("dp")
    chips = groups // 2
    capacity = 8
    slots = sources * capacity
    ff = w_in.shape[2]
    lanes = 2 * LANES
    per_row = width // capacity
    same_core = [[2 * chip + core for chip in range(chips)] for core in range(2)]
    swap = [(index, index ^ 1) for index in range(groups)]
    dp = lax.axis_index("dp")
    at = lax.axis_index("expert").astype(jnp.int32)[None]
    fold = np.zeros((LANES, LANES), np.float32)
    for lane in range(width):
        fold[lane, width + lane % per_row] = 1
    fold = jnp.asarray(fold, BF16)

    whole_block = lambda i: (0, 0)
    mine, pick = pl.pallas_call(
        functools.partial(place_kernel, capacity, experts),
        grid=(1,),
        in_specs=[
            pl.BlockSpec((2, tok_count), whole_block),
            pl.BlockSpec((width, tok_count), whole_block),
            pl.BlockSpec((width, tok_count), whole_block),
        ],
        out_specs=[
            pl.BlockSpec((slots, lanes), whole_block),
            pl.BlockSpec((slots, tok_count), whole_block),
        ],
        out_shape=(
            jax.ShapeDtypeStruct((slots, lanes), BF16),
            jax.ShapeDtypeStruct((slots, tok_count), BF16),
        ),
        compiler_params=pltpu.CompilerParams(vmem_limit_bytes=60 * 1024 * 1024),
        cost_estimate=pl.CostEstimate(
            flops=60_000_000, bytes_accessed=500_000, transcendentals=0
        ),
    )(routes.T, tokens.T, cotangent.T)
    got = lax.all_to_all(
        mine.reshape(sources, capacity, lanes), "expert", split_axis=0, concat_axis=0, tiled=True
    ).reshape(slots, lanes)

    got, w_in, w_out, router = lax.optimization_barrier((got, w_in, w_out, router))
    whole = lax.all_gather(got[None], "dp", axis=0, tiled=True)

    spare = LANES - width
    front = jnp.pad(w_in[0].reshape(groups, width, ff), ((0, 0), (0, spare), (0, 0)))
    front = front.reshape(groups * LANES, ff)
    back = jnp.pad(w_out[0].T.reshape(groups, width, ff), ((0, 0), (0, spare), (0, 0)))
    back = back.reshape(groups * LANES, ff)
    core = dp % 2

    def half(which):
        picked = [
            lax.dynamic_index_in_dim(part.reshape(chips, 2, LANES, ff), which, 1, keepdims=False)
            for part in (front, back)
        ]
        return jnp.stack(picked).reshape(2, chips * LANES, ff)

    own = half(core)
    other = lax.ppermute(half(1 - core), "dp", swap)
    scorer = jnp.pad(
        router.T.reshape(experts, groups, width), ((0, LANES - experts), (0, 0), (0, spare))
    ).reshape(LANES, groups * LANES)

    whole, other, own = lax.optimization_barrier((whole, other, own))
    both, gating, gate_term, chances = pl.pallas_call(
        functools.partial(expert_kernel, experts),
        in_specs=[SMEM, HBM, HBM, HBM, VMEM],
        out_specs=[VMEM] * 4,
        scratch_shapes=[
            pltpu.VMEM((groups, slots, lanes), BF16),
            pltpu.VMEM((groups * LANES, ff), BF16),
            pltpu.VMEM((groups * LANES, ff), BF16),
            pltpu.SemaphoreType.DMA((4,)),
        ],
        out_shape=(
            jax.ShapeDtypeStruct((2, slots, ff), BF16),
            jax.ShapeDtypeStruct((slots, LANES), F32),
            jax.ShapeDtypeStruct((8, slots), F32),
            jax.ShapeDtypeStruct((experts, slots), F32),
        ),
        compiler_params=pltpu.CompilerParams(vmem_limit_bytes=EXPERT_VMEM),
        cost_estimate=pl.CostEstimate(
            flops=3_000_000_000, bytes_accessed=16_000_000, transcendentals=slots * ff
        ),
    )(at, whole, front, back, scorer)

    both_other = lax.ppermute(both, "dp", swap)
    terms_params = dict(
        compiler_params=pltpu.CompilerParams(vmem_limit_bytes=VMEM_LIMIT),
        cost_estimate=pl.CostEstimate(
            flops=2_000_000_000, bytes_accessed=8_000_000, transcendentals=0
        ),
    )
    keep, near = pl.pallas_call(
        keep_kernel,
        in_specs=[VMEM, VMEM, VMEM, HBM],
        out_specs=[VMEM] * 2,
        out_shape=(
            jax.ShapeDtypeStruct((chips, slots, lanes), BF16),
            jax.ShapeDtypeStruct(other.shape, BF16),
        ),
        scratch_shapes=[pltpu.SemaphoreType.DMA],
        **terms_params,
    )(both, gating, own, other)
    halves = pl.pallas_call(
        other_kernel,
        in_specs=[VMEM] * 4,
        out_specs=HBM,
        out_shape=jax.ShapeDtypeStruct((chips, slots, lanes), BF16),
        scratch_shapes=[
            pltpu.VMEM((chips, slots, lanes), BF16),
            pltpu.SemaphoreType.DMA((chips // 2,)),
        ],
        **terms_params,
    )(both_other, gating, near, keep)
    halves, gate_term = lax.optimization_barrier((halves, gate_term))
    sums = lax.psum_scatter(
        halves, "dp", scatter_dimension=0, axis_index_groups=same_core, tiled=True
    )

    gates = lax.all_to_all(
        jnp.broadcast_to(gate_term[None, :1], (groups, 1, slots)),
        "dp",
        split_axis=0,
        concat_axis=0,
        tiled=True,
    ).reshape(groups, slots)
    score_grad, router_part = call(
        router_kernel,
        (
            jax.ShapeDtypeStruct((experts, slots), BF16),
            jax.ShapeDtypeStruct((experts, LANES), F32),
        ),
        [SMEM] + [VMEM] * 3,
    )(at, gates, chances, got)
    router_column = lax.all_to_all(
        router_part.reshape(experts, 1, LANES), "expert", split_axis=0, concat_axis=0, tiled=True
    ).reshape(experts, LANES)

    router_slice = lax.dynamic_slice_in_dim(router.T, dp * width, width, 1)
    router_slice = jnp.pad(router_slice, ((0, 0), (0, spare)))
    home = call(
        functools.partial(return_kernel, capacity, per_row),
        jax.ShapeDtypeStruct((slots, lanes), BF16),
        [VMEM] * 5,
    )(sums.reshape(slots, lanes), score_grad, router_slice, router_column, fold)
    home = lax.all_to_all(
        home.reshape(sources, capacity, lanes), "expert", split_axis=0, concat_axis=0, tiled=True
    ).reshape(slots, lanes)
    mixed, token_grad, router_grad = call(
        functools.partial(combine_kernel, capacity, per_row),
        (
            jax.ShapeDtypeStruct((width, tok_count), BF16),
            jax.ShapeDtypeStruct((width, tok_count), BF16),
            jax.ShapeDtypeStruct((experts, width), F32),
        ),
        [VMEM] * 3,
    )(home, pick, fold)
    return (mixed.T, token_grad.T, router_grad.T)


def solution(mesh):
    placed = (
        P("expert", "dp"),
        P("expert", "dp"),
        P("expert", None),
        P(),
        P("expert", None, "dp"),
        P("expert", "dp", None),
    )
    return jax.shard_map(
        shards,
        mesh=mesh,
        in_specs=placed,
        out_specs=(P("expert", "dp"), P("expert", "dp"), P("dp", None)),
        check_vma=False,
    )
```
